512 devices in a mesh: grp: 16 (over y, core), row: 32 (over x, z).
Axes of the slice: x: 4, y: 8, z: 8, core: 2. Of those that a mesh axis runs over, the one named last changes fastest.
Arguments:
- embeddings: bfloat16 [262144, 1024], P(('grp', 'row')), may hold values from -24 to 24
- rotation: bfloat16 [1024, 1024], replicated, may hold values from -0.1875 to 0.1875
- pq_codes: int32 [262144, 64], P(('grp', 'row')), may hold values from 0 to 255, as said below
- codebook: bfloat16 [64, 16, 256], P('row'), may hold values from -6 to 6
Outputs:
- new_codebook: bfloat16 [64, 16, 256], replicated
- rerotated: bfloat16 [262144, 1024], P(('grp', 'row'))
The draws below stay inside these ranges and needn't reach their ends.
Inputs may be any that keep to these rules, and one draw needn't show every extreme that they name: pq_codes[t, m] names one of the 256 centroids of subspace m.
All inputs are finite; a program needn't handle non-finite values.
Results may differ from the reference program's by a relative error of at most 0.025.
Values may be sent and summed in bfloat16 or wider, within the bound.
No kernel may reach another device: no remote copies, remote signals or barrier semaphores. Data moves between devices by JAX's collectives and lax.ppermute only.
A program may use at most 64 MiB of HBM per device.

```python
import jax
import jax.numpy as jnp
from jax import lax

D = 1024
M = 64
K = 256
DS = 16
TOK_DEV = 512
ITERS = 4
TOKENS = 262144


def draw_embeddings(key, part):
    key = jax.random.fold_in(key, 11)
    position = jnp.arange(D, dtype=jnp.float32) / D
    values = jnp.clip(jax.random.normal(key, (TOKENS, D), jnp.float32), -4.0, 4.0)
    column_scale = jnp.power(6.0, position)
    return (values * column_scale[None, :]).astype(jnp.bfloat16)


def draw_pq_codes(key, part):
    key = jax.random.fold_in(key, 7)
    key_parts = jax.random.split(key, 3)
    unused_count = jax.random.randint(key_parts[0], (M,), 0, K // 8 + 1)
    live_count = K - unused_count
    raw_slot = unused_count[None, :] + jax.random.randint(key_parts[1], (TOKENS, M), 0, live_count[None, :])
    orders = jax.vmap(lambda sub_key: jax.random.permutation(sub_key, K))(jax.random.split(key_parts[2], M))
    labels = jnp.take_along_axis(orders.T, raw_slot, axis=0)
    return labels.astype(jnp.int32)


def block_levels(key, extent, shards, low, largest):
    loudness = 1.0
    for axis_at, shards_of in shards:
        steps = jax.random.uniform(jax.random.fold_in(jax.random.fold_in(key, 6), axis_at), (shards_of,), jnp.float32, low / len(shards), largest / len(shards))
        loudness = loudness * jnp.repeat(jnp.exp(steps), extent[axis_at] // shards_of).reshape((-1,) + (1,) * (len(extent) - 1 - axis_at))
    return loudness


def noise(rng, extent, width, limit, cuts=(), kind=jnp.bfloat16):
    level = block_levels(rng, extent, cuts, -0.22, 0.18) if cuts else 1.0
    values = jax.random.normal(rng, extent, jnp.float32) * width * level
    return jnp.minimum(jnp.maximum(values, -limit), limit).astype(kind)


def setup_inputs(seed: int = 0) -> dict:
    streams_of = jax.random.split(jax.random.key(seed), 5)
    embeddings = draw_embeddings(jax.random.fold_in(streams_of[4], 71), 0)
    rotation = noise(streams_of[1], (D, D), D ** -0.5, 0.1875)
    pq_codes = draw_pq_codes(jax.random.fold_in(streams_of[4], 71), 0)
    codebook = noise(streams_of[3], (M, DS, K), 1.0, 6.0, ((0, 32),))
    return dict(embeddings=embeddings, rotation=rotation, pq_codes=pq_codes, codebook=codebook)


epsilon = 1e-06

def reference(embeddings, rotation, pq_codes, codebook):
    blocks = TOKENS // TOK_DEV
    sub_width = D // M
    offsets = (jnp.arange(M, dtype=jnp.int32) * K)[None, :]
    sub_index = jnp.arange(M, dtype=jnp.int32)[None, :]

    def one_block(carry, block_index):
        cross_cov, code_sums, counts = carry
        row_block = lax.dynamic_slice_in_dim(embeddings, block_index * TOK_DEV, TOK_DEV, 0)
        labels = lax.dynamic_slice_in_dim(pq_codes, block_index * TOK_DEV, TOK_DEV, 0)
        rotated = jnp.dot(row_block, rotation, preferred_element_type=jnp.float32).astype(jnp.bfloat16)
        rebuilt = codebook[sub_index, :, labels].reshape(TOK_DEV, D)
        partial_cross = lax.dot_general(row_block, rebuilt, (((0,), (0,)), ((), ())), preferred_element_type=jnp.float32)
        rounded = lax.optimization_barrier(partial_cross.astype(jnp.bfloat16)).astype(jnp.float32)
        segment = (labels + offsets).reshape(-1)
        values = rotated.astype(jnp.float32).reshape(TOK_DEV * M, sub_width)
        code_sums = code_sums + jax.ops.segment_sum(values, segment, num_segments=M * K)
        counts = counts + jax.ops.segment_sum(jnp.ones((TOK_DEV * M,), jnp.float32), segment, num_segments=M * K)
        return ((cross_cov + rounded, code_sums, counts), None)
    initial = (jnp.zeros((D, D), jnp.float32), jnp.zeros((M * K, sub_width), jnp.float32), jnp.zeros((M * K,), jnp.float32))
    (cross_cov, code_sums, counts), unused = lax.scan(one_block, initial, jnp.arange(blocks, dtype=jnp.int32))
    code_sums = code_sums.reshape(M, K, sub_width).transpose(0, 2, 1)
    counts = counts.reshape(M, K)
    refreshed = jnp.where(counts[:, None, :] > 0, code_sums / jnp.maximum(counts, 1.0)[:, None, :], codebook.astype(jnp.float32)).astype(jnp.bfloat16)
    packed_cross = cross_cov.astype(jnp.bfloat16)
    gram_matrix = jnp.dot(packed_cross, packed_cross.T, preferred_element_type=jnp.float32)
    norm_square = jnp.sqrt(jnp.sum(jnp.square(gram_matrix))) + epsilon
    inverse = 1.0 / jnp.sqrt(norm_square)
    weights = (gram_matrix / norm_square).astype(jnp.bfloat16)
    polar_iter = 1.5 * inverse * cross_cov - 0.5 * inverse * jnp.dot(weights, packed_cross, preferred_element_type=jnp.float32)
    for turn_index in range(ITERS - 1):
        packed_polar = polar_iter.astype(jnp.bfloat16)
        weights = jnp.dot(packed_polar, packed_polar.T, preferred_element_type=jnp.float32).astype(jnp.bfloat16)
        polar_iter = 1.5 * polar_iter - 0.5 * jnp.dot(weights, packed_polar, preferred_element_type=jnp.float32)
    new_rotation = polar_iter.astype(jnp.bfloat16)

    def rotate_block(row_block):
        return jnp.dot(row_block, new_rotation, preferred_element_type=jnp.float32).astype(jnp.bfloat16)
    rerotated = lax.map(rotate_block, embeddings.reshape(blocks, TOK_DEV, D)).reshape(TOKENS, D)
    return (refreshed, rerotated)
```

```python
import jax
import jax.numpy as jnp
from jax import lax
from jax.sharding import Mesh, PartitionSpec as P

ITERS = 4
EPSILON = 1e-06
F32 = jnp.float32
BF16 = jnp.bfloat16

AXES = ("yh", "yl", "core", "x", "zh", "zl")
ROW = ("x", "zh", "zl")
BOX = ("x", "yl", "zl")
FAR = ("yh", "zh")
LEVEL = 256.0


def gather(value, axes, peers):
    return lax.all_to_all(
        jnp.broadcast_to(value[None], (peers,) + value.shape), axes, 0, 0, tiled=True
    )


def spread(parts, axes):
    return jnp.sum(lax.all_to_all(parts, axes, 0, 0, tiled=True).astype(F32), axis=0)


def one_hot(code_block, centroids):
    levels = lax.broadcasted_iota(jnp.int32, (1, 1, centroids), 2)
    return (code_block[:, :, None] == levels).astype(BF16)


def rebuild(pq_codes, full_book, rotated):
    tokens, subspaces = pq_codes.shape
    sub_width = full_book.shape[1]
    centroids = full_book.shape[2]
    stride = min(subspaces, 16)
    pieces = []
    sum_parts = []
    count_parts = []
    for first_sub in range(0, subspaces, stride):
        last_sub = first_sub + stride
        one_hots = one_hot(pq_codes[:, first_sub:last_sub], centroids)
        picked = jnp.einsum(
            "tmk,mdk->tmd",
            one_hots,
            full_book[first_sub:last_sub],
            preferred_element_type=F32,
        )
        pieces.append(picked.reshape(tokens, stride * sub_width).astype(BF16))
        sub_view = rotated[:, first_sub * sub_width : last_sub * sub_width].reshape(
            tokens, stride, sub_width
        )
        sum_parts.append(
            jnp.einsum("tmd,tmk->mdk", sub_view, one_hots, preferred_element_type=F32)
        )
        count_parts.append(jnp.sum(one_hots, axis=0, dtype=F32))
    rebuilt = jnp.concatenate(pieces, axis=1)
    return rebuilt, jnp.concatenate(sum_parts, axis=0), jnp.concatenate(count_parts, axis=0)


def digits(counts):
    high = jnp.floor(counts * (1.0 / LEVEL))
    return counts - LEVEL * high, high


def count_rows(counts):
    low, high = digits(counts)
    rows = jnp.concatenate([low, high], axis=1).reshape(-1, 4, 128)
    return jnp.pad(rows, ((0, 0), (0, 4), (0, 0))).reshape(-1, 128)


def counts_of(rows):
    both = rows.reshape(-1, 8, 128)[:, :4].reshape(-1, 512)
    return both[:, :256] + LEVEL * both[:, 256:]


def polar_of(cross):
    polar = cross.astype(F32)
    for turn in range(ITERS):
        packed = polar.astype(BF16)
        gram = lax.dot_general(packed, packed, (((1,), (1,)), ((), ())), preferred_element_type=F32)
        scale = 1.0
        if turn == 0:
            norm_square = jnp.sqrt(jnp.sum(jnp.square(gram))) + EPSILON
            scale = 1.0 / jnp.sqrt(norm_square)
            gram = gram / norm_square
        step = jnp.dot(gram.astype(BF16), packed, preferred_element_type=F32)
        polar = (1.5 * scale) * polar - (0.5 * scale) * step
    return polar.astype(BF16)


def local(embeddings, rotation, pq_codes, codebook):
    full_book = gather(codebook, ROW, 32).reshape(64, 16, 256)
    rotated = jnp.dot(embeddings, rotation, preferred_element_type=F32).astype(BF16)
    rebuilt, sums, counts = rebuild(pq_codes, full_book, rotated)
    cross = lax.dot_general(
        embeddings, rebuilt, (((0,), (0,)), ((), ())), preferred_element_type=F32
    ).astype(BF16)
    sums = sums.astype(BF16)
    payload = jnp.concatenate(
        [
            cross[:512],
            cross[512:],
            sums[:, :8].reshape(512, 256),
            sums[:, 8:].reshape(512, 256),
            count_rows(counts).astype(BF16),
        ],
        axis=1,
    )

    def repack(total):
        counted = count_rows(counts_of(total[:, 2560:]))
        return jnp.concatenate([total[:, :2560], counted], axis=1).astype(BF16)

    pair = repack(spread(payload.reshape(2, 256, 2688), "core"))
    boxed = spread(pair.reshape(16, 16, 2688), BOX)
    low, high = digits(counts_of(boxed[:, 2560:]))
    counted = jnp.repeat(jnp.concatenate([low, high], axis=1), 8, axis=0)
    far = jnp.concatenate([boxed[:, :2560], counted], axis=1).astype(BF16)
    total = spread(far.reshape(16, 24, 128), FAR)

    owner = lax.axis_index("core") * 256 + lax.axis_index(BOX) * 16 + lax.axis_index(FAR)
    old = lax.dynamic_slice_in_dim(full_book, owner // 8, 1, 0)[0]
    old = jnp.concatenate(
        [
            lax.dynamic_slice_in_dim(old, owner % 8, 1, 0),
            lax.dynamic_slice_in_dim(old, owner % 8 + 8, 1, 0),
        ],
        axis=0,
    ).astype(F32)
    own_sums = total[16:20].reshape(2, 256)
    own_counts = total[20:22].reshape(1, 256) + LEVEL * total[22:24].reshape(1, 256)
    fresh = jnp.where(own_counts > 0, own_sums / jnp.maximum(own_counts, 1.0), old)
    own = jnp.concatenate([total[:16], fresh.reshape(4, 128)], axis=0).astype(BF16)

    rows = gather(own, FAR, 16).reshape(16, 2560)
    rows = gather(rows, BOX, 16).reshape(256, 2560)
    rows = gather(rows, "core", 2).reshape(512, 2560)
    cross = jnp.concatenate([rows[:, :1024], rows[:, 1024:2048]], axis=0)
    new_codebook = jnp.concatenate(
        [rows[:, 2048:2304].reshape(64, 8, 256), rows[:, 2304:].reshape(64, 8, 256)], axis=1
    )
    rerotated = jnp.dot(embeddings, polar_of(cross), preferred_element_type=F32)
    return (new_codebook, rerotated.astype(BF16))


def solution(mesh):
    split = Mesh(mesh.devices.reshape(4, 2, 2, 4, 4, 2), AXES)
    placed = (P(AXES, None), P(), P(AXES, None), P(ROW, None, None))
    return jax.shard_map(
        local, mesh=split, in_specs=placed, out_specs=(P(), P(AXES, None)), check_vma=False
    )
```

```python
import functools

import jax
import jax.numpy as jnp
from jax import lax
from jax.experimental import pallas as pl
from jax.experimental.pallas import tpu as pltpu
from jax.sharding import Mesh, PartitionSpec as P

ITERS = 4
EPSILON = 1e-06
F32 = jnp.float32
BF16 = jnp.bfloat16

AXES = ("yh", "yl", "core", "x", "zh", "zl")
ROW = ("x", "zh", "zl")
BOX = ("x", "yl", "zl")
FAR = ("yh", "zh")

D = 1024
SUBS = 64
HALF = SUBS // 2
DS = 16
K = 256
TOK = 512
LOW = 64.0
WIDE = 2 * D + 2 * K + 128
BACK = 2 * D + 2 * K

NN = (((1,), (0,)), ((), ()))
NT = (((1,), (1,)), ((), ()))
PARAMS = pltpu.CompilerParams(vmem_limit_bytes=56 * 1024 * 1024)


def dot(a, b, dims=NN):
    return lax.dot_general(a, b, dims, preferred_element_type=F32)


def whole():
    return pl.BlockSpec(memory_space=pltpu.VMEM)


def gather(value, axes, peers):
    return lax.all_to_all(
        jnp.broadcast_to(value[None], (peers,) + value.shape), axes, 0, 0, tiled=True
    )


def spread(parts, axes):
    return jnp.sum(lax.all_to_all(parts, axes, 0, 0, tiled=True).astype(F32), axis=0)


def picks(codes_ref, sub):
    row = codes_ref[pl.ds(sub, 1), :]
    levels = lax.broadcasted_iota(jnp.int32, (K, TOK), 0)
    return jnp.where(levels == row, 1.0, 0.0).astype(BF16)


def tables_kernel(emb_ref, rot_ref, codes_ref, out_ref, turned_ref):
    def turn(tile, carry):
        rows = pl.ds(pl.multiple_of(tile * 128, 128), 128)
        rotated = dot(emb_ref[rows, :], rot_ref[...])
        turned_ref[:, rows] = rotated.T.astype(BF16)
        return carry

    lax.fori_loop(0, TOK // 128, turn, 0)
    ones = jnp.ones((DS, TOK), BF16)
    line = lax.broadcasted_iota(jnp.int32, (DS, 128), 0)

    def one(sub):
        at = pl.ds(pl.multiple_of(sub * DS, DS), DS)
        left = jnp.concatenate([turned_ref[at, :], ones], axis=0)
        both = dot(left, picks(codes_ref, sub), NT)
        counts = both[DS:]
        high = jnp.floor(counts * (1.0 / LOW))
        return both[:DS], counts - LOW * high, high

    def step(pair, carry):
        at = pl.ds(pl.multiple_of(pair * DS, DS), DS)
        digits = jnp.zeros((DS, 128), F32)
        for half in range(2):
            sums, low, high = one(pair + HALF * half)
            out_ref[at, K * half : K * half + K] = sums.astype(BF16)
            for place, part in enumerate((low[:, :128], low[:, 128:], high[:, :128], high[:, 128:])):
                digits = jnp.where(line == 4 * half + place, part, digits)
        out_ref[at, 2 * K :] = digits.astype(BF16)
        return carry

    lax.fori_loop(0, HALF, step, 0, unroll=4)


def tables(embeddings, rotation, codes):
    return pl.pallas_call(
        tables_kernel,
        out_shape=jax.ShapeDtypeStruct((TOK, 2 * K + 128), BF16),
        in_specs=[whole()] * 3,
        out_specs=whole(),
        scratch_shapes=[pltpu.VMEM((D, TOK), BF16)],
        compiler_params=PARAMS,
        cost_estimate=pl.CostEstimate(flops=8 * 10**9, bytes_accessed=4 * 10**6, transcendentals=0),
        name="tables",
    )(embeddings, rotation, codes)


def cross_kernel(emb_ref, codes_ref, book_ref, table_ref, out_ref, rebuilt_ref):
    def step(sub, carry):
        at = pl.ds(pl.multiple_of(sub * DS, DS), DS)
        rebuilt_ref[at, :] = dot(book_ref[at, :], picks(codes_ref, sub)).astype(BF16)
        return carry

    lax.fori_loop(0, SUBS, step, 0, unroll=8)
    out_ref[:, 2 * D :] = table_ref[...]
    for side in range(2):

        def tile(i, carry):
            here = pl.multiple_of(i * 128, 128)
            part = dot(rebuilt_ref[pl.ds(side * TOK + here, 128), :], emb_ref[...])
            out_ref[pl.ds(here, 128), side * D : side * D + D] = part.astype(BF16)
            return carry

        lax.fori_loop(0, TOK // 128, tile, 0)


def crosses(embeddings, codes, book, table):
    return pl.pallas_call(
        cross_kernel,
        out_shape=jax.ShapeDtypeStruct((TOK, WIDE), BF16),
        in_specs=[whole()] * 4,
        out_specs=whole(),
        scratch_shapes=[pltpu.VMEM((D, TOK), BF16)],
        compiler_params=PARAMS,
        cost_estimate=pl.CostEstimate(flops=8 * 10**9, bytes_accessed=6 * 10**6, transcendentals=0),
        name="crosses",
    )(embeddings, codes, book, table)


TILE = 256


def polar_kernel(rows_ref, emb_ref, out_ref, book_ref, a_ref, b_ref, gram_ref, full_ref, polar_ref):
    book_ref[:TOK, :] = rows_ref[:, 2 * D : 2 * D + K]
    book_ref[TOK:, :] = rows_ref[:, 2 * D + K : 2 * D + 2 * K]
    a_ref[:TOK, :] = rows_ref[:, :D]
    a_ref[TOK:, :] = rows_ref[:, D : 2 * D]

    def tiles(body, init):
        def run(i, carry):
            return body(pl.ds(pl.multiple_of(i * TILE, TILE), TILE), carry)

        return lax.fori_loop(0, D // TILE, run, init)

    def first_gram(at, total):
        part = dot(a_ref[at, :], a_ref[...], NT)
        full_ref[at, :] = part
        return total + jnp.sum((part * part).reshape(TILE // 8, 8, D), axis=0)

    squares = tiles(first_gram, jnp.zeros((8, D), F32))
    norm_square = jnp.sqrt(jnp.sum(squares, keepdims=True)) + EPSILON
    scale = lax.rsqrt(norm_square)

    def first_step(at, carry):
        weights = (full_ref[at, :] / norm_square).astype(BF16)
        part = (1.5 * scale) * a_ref[at, :].astype(F32) - (0.5 * scale) * dot(weights, a_ref[...])
        polar_ref[at, :] = part
        b_ref[at, :] = part.astype(BF16)
        return carry

    tiles(first_step, 0)
    now, later = b_ref, a_ref
    for turn in range(1, ITERS):

        def advance(at, carry, now=now, later=later, turn=turn):
            gram = dot(now[at, :], now[...], NT).astype(BF16)
            part = 1.5 * polar_ref[at, :] - 0.5 * dot(gram, now[...])
            if turn < ITERS - 1:
                polar_ref[at, :] = part
            later[at, :] = part.astype(BF16)
            return carry

        tiles(advance, 0)
        now, later = later, now

    def rotate(i, carry):
        at = pl.ds(pl.multiple_of(i * TILE, TILE), TILE)
        out_ref[at, :] = dot(emb_ref[at, :], now[...], NT).astype(BF16)
        return carry

    lax.fori_loop(0, TOK // TILE, rotate, 0)


def finish(rows, embeddings):
    return pl.pallas_call(
        polar_kernel,
        out_shape=(
            jax.ShapeDtypeStruct((TOK, D), BF16),
            jax.ShapeDtypeStruct((SUBS * DS, K), BF16),
        ),
        in_specs=[whole()] * 2,
        out_specs=(whole(),) * 2,
        scratch_shapes=[
            pltpu.VMEM((D, D), BF16),
            pltpu.VMEM((D, D), BF16),
            pltpu.VMEM((8, 128), BF16),
            pltpu.VMEM((D, D), F32),
            pltpu.VMEM((D, D), F32),
        ],
        compiler_params=PARAMS,
        cost_estimate=pl.CostEstimate(flops=20 * 10**9, bytes_accessed=8 * 10**6, transcendentals=0),
        name="polar",
    )(rows, embeddings)


def local(embeddings, rotation, pq_codes, codebook):
    codes = pq_codes.T
    full_book = gather(codebook, ROW, 32).reshape(SUBS * DS, K)
    table = tables(embeddings, rotation, codes)
    payload = crosses(embeddings, codes, full_book, table)

    pair = spread(payload.reshape(2, 256, WIDE), "core").astype(BF16)
    boxed = spread(pair.reshape(16, 16, WIDE), BOX)
    counted = boxed[:8, BACK:].reshape(2, 2, 256)
    counted = counted[:, 0] + LOW * counted[:, 1]
    high = jnp.floor(counted * (1.0 / 256.0))
    digits = jnp.concatenate([counted - 256.0 * high, high], axis=0).reshape(1, 8, 128)
    far = jnp.concatenate(
        [
            boxed[:, :BACK].reshape(16, 20, 128),
            jnp.broadcast_to(digits, (16, 8, 128)),
            jnp.zeros((16, 4, 128), F32),
        ],
        axis=1,
    ).astype(BF16)
    total = spread(far, FAR)

    owner = lax.axis_index("core") * 256 + lax.axis_index(BOX) * 16 + lax.axis_index(FAR)
    old = jnp.concatenate(
        [lax.dynamic_slice_in_dim(full_book, owner + TOK * half, 1, 0) for half in range(2)], axis=0
    ).astype(F32)
    own_sums = total[16:20].reshape(2, K)
    own_counts = total[20:24].reshape(2, K) + 256.0 * total[24:28].reshape(2, K)
    fresh = jnp.where(own_counts > 0, own_sums / jnp.maximum(own_counts, 1.0), old)
    own = jnp.concatenate([total[:16], fresh.reshape(4, 128)], axis=0).astype(BF16)

    rows = gather(own, FAR, 16).reshape(16, BACK)
    rows = gather(rows, BOX, 16).reshape(256, BACK)
    rows = gather(rows, "core", 2).reshape(512, BACK)
    rerotated, new_codebook = finish(rows, embeddings)
    return (new_codebook.reshape(SUBS, DS, K), rerotated)


def solution(mesh):
    split = Mesh(mesh.devices.reshape(4, 2, 2, 4, 4, 2), AXES)
    placed = (P(AXES, None), P(), P(AXES, None), P(ROW, None, None))
    return jax.shard_map(
        local, mesh=split, in_specs=placed, out_specs=(P(), P(AXES, None)), check_vma=False
    )
```

```python
import jax
import jax.numpy as jnp
from jax import lax
from jax.experimental import pallas as pl
from jax.experimental.pallas import tpu as pltpu
from jax.sharding import Mesh, PartitionSpec as P

ITERS = 4
EPSILON = 1e-06
F32 = jnp.float32
BF16 = jnp.bfloat16

AXES = ("yh", "yl", "core", "x", "zh", "zl")
ROW = ("x", "zh", "zl")
NEAR = ("x", "zl")
FAR = ("yh", "yl", "zh")

D = 1024
SUBS = 64
HALF = SUBS // 2
QUARTER = SUBS // 4
DS = 16
K = 256
TOK = 512
MINE = TOK // 2
LOW = 64.0
BACK = 2 * D + 2 * K
WIDE = BACK + 128

NN = (((1,), (0,)), ((), ()))
NT = (((1,), (1,)), ((), ()))
PARAMS = pltpu.CompilerParams(vmem_limit_bytes=56 * 1024 * 1024)
VMEM = pl.BlockSpec(memory_space=pltpu.VMEM)
SMEM = pl.BlockSpec(memory_space=pltpu.SMEM)


def dot(a, b, dims=NN):
    return lax.dot_general(a, b, dims, preferred_element_type=F32)


def gather(value, axes, peers):
    return lax.all_to_all(
        jnp.broadcast_to(value[None], (peers,) + value.shape), axes, 0, 0, tiled=True
    )


def spread(parts, axes):
    return jnp.sum(lax.all_to_all(parts, axes, 0, 0, tiled=True).astype(F32), axis=0)


def swap(value):
    return lax.ppermute(value, "core", [(0, 1), (1, 0)])


def picks(codes_ref, sub):
    row = codes_ref[pl.ds(sub, 1), :]
    levels = lax.broadcasted_iota(jnp.int32, (K, TOK), 0)
    return jnp.where(levels == row, 1.0, 0.0).astype(BF16)


def tables_kernel(emb_ref, rot_ref, codes_ref, out_ref, turned_ref):
    turned_ref[...] = dot(emb_ref[...], rot_ref[...]).astype(BF16).T
    ones = jnp.ones((DS, TOK), BF16)
    line = lax.broadcasted_iota(jnp.int32, (DS, 128), 0)

    def one(sub):
        at = pl.ds(pl.multiple_of(sub * DS, DS), DS)
        left = jnp.concatenate([turned_ref[at, :], ones], axis=0)
        both = dot(left, picks(codes_ref, sub), NT)
        counts = both[DS:]
        high = jnp.floor(counts * (1.0 / LOW))
        return both[:DS], counts - LOW * high, high

    def step(q, carry):
        at = pl.ds(pl.multiple_of(q * DS, DS), DS)
        for side in range(2):
            digits = jnp.zeros((DS, 128), F32)
            for half in range(2):
                sums, low, high = one(2 * (q + QUARTER * half) + side)
                out_ref[side, at, K * half : K * half + K] = sums.astype(BF16)
                parts = (low[:, :128], low[:, 128:], high[:, :128], high[:, 128:])
                for place, part in enumerate(parts):
                    digits = jnp.where(line == 4 * half + place, part, digits)
            out_ref[side, at, 2 * K :] = digits.astype(BF16)
        return carry

    lax.fori_loop(0, QUARTER, step, 0, unroll=2)


def tables(embeddings, rotation, codes):
    return pl.pallas_call(
        tables_kernel,
        out_shape=jax.ShapeDtypeStruct((2, MINE, 2 * K + 128), BF16),
        in_specs=[VMEM] * 3,
        out_specs=VMEM,
        scratch_shapes=[pltpu.VMEM((D, TOK), BF16)],
        compiler_params=PARAMS,
        cost_estimate=pl.CostEstimate(flops=8 * 10**9, bytes_accessed=4 * 10**6, transcendentals=0),
        name="tables",
    )(embeddings, rotation, codes)


def cross_kernel(side_ref, emb_ref, codes_ref, book_ref, table_ref, out_ref, rebuilt_ref):
    side = side_ref[0]

    def step(q, carry):
        at = pl.ds(pl.multiple_of(q * DS, DS), DS)
        rebuilt_ref[at, :] = dot(book_ref[at, :], picks(codes_ref, 2 * q + side)).astype(BF16)
        return carry

    lax.fori_loop(0, HALF, step, 0, unroll=8)
    part = dot(rebuilt_ref[...], emb_ref[...])
    out_ref[:, :D] = part[:MINE].astype(BF16)
    out_ref[:, D : 2 * D] = part[MINE:].astype(BF16)
    out_ref[:, 2 * D :] = table_ref[side]


def crosses(side, embeddings, codes, book, table):
    return pl.pallas_call(
        cross_kernel,
        out_shape=jax.ShapeDtypeStruct((MINE, WIDE), BF16),
        in_specs=[SMEM] + [VMEM] * 4,
        out_specs=VMEM,
        scratch_shapes=[pltpu.VMEM((TOK, TOK), BF16)],
        compiler_params=PARAMS,
        cost_estimate=pl.CostEstimate(flops=4 * 10**9, bytes_accessed=4 * 10**6, transcendentals=0),
        name="crosses",
    )(side, embeddings, codes, book, table)


def gram_of(y_ref, gram_ref, squares=False):
    mid = D // 2
    top = dot(y_ref[:mid, :], y_ref[...], NT)
    low = dot(y_ref[mid:, :], y_ref[mid:, :], NT)
    gram_ref[:mid, :] = top.astype(BF16)
    gram_ref[mid:, :mid] = top[:, mid:].astype(BF16).T
    gram_ref[mid:, mid:] = low.astype(BF16)
    if squares:
        left, right = top[:, :mid], top[:, mid:]
        return jnp.sum(left * left + 2.0 * (right * right) + low * low, keepdims=True)
    return None


def polar_kernel(side_ref, mine_ref, other_ref, emb_ref, out_ref, book_ref, a_ref, b_ref, gram_ref, polar_ref):
    side = side_ref[0]
    for rows_ref, at in ((mine_ref, side), (other_ref, 1 - side)):
        for q in range(HALF):
            here = pl.ds((q % QUARTER) * DS, DS)
            left = (q // QUARTER) * D
            a_ref[pl.ds(pl.multiple_of((2 * q + at) * DS, DS), DS), :] = rows_ref[here, left : left + D]
            left = 2 * D + (q // QUARTER) * K
            book_ref[2 * q + at] = rows_ref[here, left : left + K]

    blocks = [pl.ds(i * (D // 2), D // 2) for i in range(2)]
    norm_square = jnp.sqrt(gram_of(a_ref, gram_ref, squares=True)) + EPSILON
    scale = lax.rsqrt(norm_square)
    for at in blocks:
        moved = dot(gram_ref[at, :], a_ref[...])
        part = (1.5 * scale) * a_ref[at, :].astype(F32) - (0.5 * scale / norm_square) * moved
        polar_ref[at, :] = part
        b_ref[at, :] = part.astype(BF16)
    now, later = b_ref, a_ref
    for turn in range(1, ITERS - 1):
        gram_of(now, gram_ref)
        for at in blocks:
            part = 1.5 * polar_ref[at, :] - 0.5 * dot(gram_ref[at, :], now[...])
            if turn < ITERS - 2:
                polar_ref[at, :] = part
            later[at, :] = part.astype(BF16)
        now, later = later, now
    gram_of(now, gram_ref)
    turned = dot(emb_ref[...], now[...], NT)
    out_ref[...] = (1.5 * turned - 0.5 * dot(turned.astype(BF16), gram_ref[...])).astype(BF16)


def finish(side, mine, other, embeddings):
    return pl.pallas_call(
        polar_kernel,
        out_shape=(
            jax.ShapeDtypeStruct((TOK, D), BF16),
            jax.ShapeDtypeStruct((SUBS, DS, K), BF16),
        ),
        in_specs=[SMEM] + [VMEM] * 3,
        out_specs=(VMEM,) * 2,
        scratch_shapes=[
            pltpu.VMEM((D, D), BF16),
            pltpu.VMEM((D, D), BF16),
            pltpu.VMEM((D, D), BF16),
            pltpu.VMEM((D, D), F32),
        ],
        compiler_params=PARAMS,
        cost_estimate=pl.CostEstimate(flops=20 * 10**9, bytes_accessed=8 * 10**6, transcendentals=0),
        name="polar",
    )(side, mine, other, embeddings)


def local(embeddings, rotation, pq_codes, codebook):
    codes = pq_codes.T
    core = lax.axis_index("core")
    mine, other = jnp.full((1,), core, jnp.int32), jnp.full((1,), 1 - core, jnp.int32)

    theirs = lax.dynamic_index_in_dim(codebook, 1 - core, 0, keepdims=False)
    other_book = gather(theirs, ROW, HALF).reshape(HALF * DS, K)
    table = tables(embeddings, rotation, codes)
    mine_book = swap(other_book)
    sent = crosses(other, embeddings, codes, other_book, table)
    got = swap(sent)
    kept = crosses(mine, embeddings, codes, mine_book, table)

    pair = (got.astype(F32) + kept.astype(F32)).astype(BF16)
    near = spread(pair.reshape(8, 32, WIDE), NEAR)
    counted = near[:, BACK:].reshape(2, 16, 128)[:, :8].reshape(2, 2, 2, K)
    counted = counted[:, :, 0] + LOW * counted[:, :, 1]
    high = jnp.floor(counted * (1.0 / 256.0))
    digits = jnp.concatenate([counted - 256.0 * high, high], axis=1).reshape(2, 1, 8, 128)
    far = jnp.concatenate(
        [
            near[:, :BACK].reshape(32, 20, 128),
            jnp.broadcast_to(digits, (2, 16, 8, 128)).reshape(32, 8, 128),
            jnp.zeros((32, 4, 128), F32),
        ],
        axis=1,
    ).astype(BF16)
    total = spread(far, FAR)

    owner = lax.axis_index(NEAR) * 32 + lax.axis_index(FAR)
    old = jnp.concatenate(
        [lax.dynamic_slice_in_dim(mine_book, owner + MINE * half, 1, 0) for half in range(2)], axis=0
    ).astype(F32)
    own_sums = total[16:20].reshape(2, K)
    own_counts = total[20:24].reshape(2, K) + 256.0 * total[24:28].reshape(2, K)
    fresh = jnp.where(own_counts > 0, own_sums / jnp.maximum(own_counts, 1.0), old)
    own = jnp.concatenate([total[:16], fresh.reshape(4, 128)], axis=0).astype(BF16)

    rows = gather(own, FAR, 32).reshape(32, BACK)
    rows = gather(rows, NEAR, 8).reshape(MINE, BACK)
    rerotated, new_codebook = finish(mine, rows, swap(rows), embeddings)
    return (new_codebook, rerotated)


def solution(mesh):
    split = Mesh(mesh.devices.reshape(4, 2, 2, 4, 4, 2), AXES)
    placed = (P(AXES, None), P(), P(AXES, None), P(ROW, None, None))
    return jax.shard_map(
        local, mesh=split, in_specs=placed, out_specs=(P(), P(AXES, None)), check_vma=False
    )
```

```python
import jax
import jax.numpy as jnp
from jax import lax
from jax.experimental import pallas as pl
from jax.experimental.pallas import tpu as pltpu
from jax.sharding import Mesh, PartitionSpec as P

ITERS = 4
EPSILON = 1e-06
F32 = jnp.float32
BF16 = jnp.bfloat16

AXES = ("yh", "yl", "core", "x", "zh", "zl")
ROW = ("x", "zh", "zl")
BOX = ("x", "yl", "zl")

D = 1024
SUBS = 64
HALF = SUBS // 2
QUARTER = SUBS // 4
DS = 16
K = 256
TOK = 512
MINE = TOK // 2
LOW = 64.0
BACK = 2 * D + 2 * K
WIDE = BACK + 128

NN = (((1,), (0,)), ((), ()))
NT = (((1,), (1,)), ((), ()))
MIB = 1024 * 1024
VMEM = pl.BlockSpec(memory_space=pltpu.VMEM)
SMEM = pl.BlockSpec(memory_space=pltpu.SMEM)


def dot(a, b, dims=NN):
    return lax.dot_general(a, b, dims, preferred_element_type=F32)


def gather(value, axes, peers):
    return lax.all_to_all(
        jnp.broadcast_to(value[None], (peers,) + value.shape), axes, 0, 0, tiled=True
    )


def spread(parts, axes):
    return jnp.sum(lax.all_to_all(parts, axes, 0, 0, tiled=True).astype(F32), axis=0)


def total(value, axes, peers):
    return jnp.sum(gather(value, axes, peers).astype(F32), axis=0)


def swap(value):
    return lax.ppermute(value, "core", [(0, 1), (1, 0)])


def picks(codes_ref, sub):
    row = codes_ref[pl.ds(sub, 1), :]
    levels = lax.broadcasted_iota(jnp.int32, (K, TOK), 0)
    return jnp.where(levels == row, 1.0, 0.0).astype(BF16)


def tables_kernel(emb_ref, rot_ref, codes_ref, out_ref, turned_ref):
    turned_ref[...] = dot(emb_ref[...], rot_ref[...]).astype(BF16).T
    ones = jnp.ones((DS, TOK), BF16)
    line = lax.broadcasted_iota(jnp.int32, (DS, 128), 0)

    def one(sub):
        at = pl.ds(pl.multiple_of(sub * DS, DS), DS)
        left = jnp.concatenate([turned_ref[at, :], ones], axis=0)
        both = dot(left, picks(codes_ref, sub), NT)
        counts = both[DS:]
        high = jnp.floor(counts * (1.0 / LOW))
        return both[:DS], counts - LOW * high, high

    def step(q, carry):
        at = pl.ds(pl.multiple_of(q * DS, DS), DS)
        for side in range(2):
            digits = jnp.zeros((DS, 128), F32)
            for half in range(2):
                sums, low, high = one(2 * (q + QUARTER * half) + side)
                out_ref[side, at, K * half : K * half + K] = sums.astype(BF16)
                parts = (low[:, :128], low[:, 128:], high[:, :128], high[:, 128:])
                for place, part in enumerate(parts):
                    digits = jnp.where(line == 4 * half + place, part, digits)
            out_ref[side, at, 2 * K :] = digits.astype(BF16)
        return carry

    lax.fori_loop(0, QUARTER, step, 0, unroll=2)


def tables(embeddings, rotation, codes):
    return pl.pallas_call(
        tables_kernel,
        out_shape=jax.ShapeDtypeStruct((2, MINE, 2 * K + 128), BF16),
        in_specs=[VMEM] * 3,
        out_specs=VMEM,
        scratch_shapes=[pltpu.VMEM((D, TOK), BF16)],
        compiler_params=pltpu.CompilerParams(vmem_limit_bytes=20 * MIB),
        cost_estimate=pl.CostEstimate(flops=8 * 10**9, bytes_accessed=4 * 10**6, transcendentals=0),
        name="tables",
    )(embeddings, rotation, codes)


def cross_kernel(side_ref, emb_ref, codes_ref, book_ref, table_ref, out_ref, rebuilt_ref):
    side = side_ref[0]

    def step(q, carry):
        at = pl.ds(pl.multiple_of(q * DS, DS), DS)
        rebuilt_ref[at, :] = dot(book_ref[at, :], picks(codes_ref, 2 * q + side)).astype(BF16)
        return carry

    lax.fori_loop(0, HALF, step, 0, unroll=8)
    part = dot(rebuilt_ref[...], emb_ref[...])
    out_ref[:, :D] = part[:MINE].astype(BF16)
    out_ref[:, D : 2 * D] = part[MINE:].astype(BF16)
    out_ref[:, 2 * D :] = table_ref[side]


def crosses(side, embeddings, codes, book, table):
    return pl.pallas_call(
        cross_kernel,
        out_shape=jax.ShapeDtypeStruct((MINE, WIDE), BF16),
        in_specs=[SMEM] + [VMEM] * 4,
        out_specs=VMEM,
        scratch_shapes=[pltpu.VMEM((TOK, TOK), BF16)],
        compiler_params=pltpu.CompilerParams(vmem_limit_bytes=16 * MIB),
        cost_estimate=pl.CostEstimate(flops=4 * 10**9, bytes_accessed=4 * 10**6, transcendentals=0),
        name="crosses",
    )(side, embeddings, codes, book, table)


def gram_of(y_ref, gram_ref, squares=False):
    mid = D // 2
    top = dot(y_ref[:mid, :], y_ref[...], NT)
    low = dot(y_ref[mid:, :], y_ref[mid:, :], NT)
    gram_ref[:mid, :] = top.astype(BF16)
    gram_ref[mid:, :mid] = top[:, mid:].astype(BF16).T
    gram_ref[mid:, mid:] = low.astype(BF16)
    if squares:
        left, right = top[:, :mid], top[:, mid:]
        return jnp.sum(left * left + 2.0 * (right * right) + low * low, keepdims=True)
    return None


def polar_kernel(side_ref, mine_ref, other_ref, emb_ref, out_ref, book_ref, a_ref, b_ref, gram_ref, polar_ref):
    side = side_ref[0]
    for rows_ref, at in ((mine_ref, side), (other_ref, 1 - side)):
        for q in range(HALF):
            here = pl.ds((q % QUARTER) * DS, DS)
            left = (q // QUARTER) * D
            a_ref[pl.ds(pl.multiple_of((2 * q + at) * DS, DS), DS), :] = rows_ref[here, left : left + D]
            left = 2 * D + (q // QUARTER) * K
            book_ref[2 * q + at] = rows_ref[here, left : left + K]

    blocks = [pl.ds(i * (D // 2), D // 2) for i in range(2)]
    norm_square = jnp.sqrt(gram_of(a_ref, gram_ref, squares=True)) + EPSILON
    scale = lax.rsqrt(norm_square)
    for at in blocks:
        moved = dot(gram_ref[at, :], a_ref[...])
        part = (1.5 * scale) * a_ref[at, :].astype(F32) - (0.5 * scale / norm_square) * moved
        polar_ref[at, :] = part
        b_ref[at, :] = part.astype(BF16)
    now, later = b_ref, a_ref
    for turn in range(1, ITERS - 1):
        gram_of(now, gram_ref)
        for at in blocks:
            part = 1.5 * polar_ref[at, :] - 0.5 * dot(gram_ref[at, :], now[...])
            if turn < ITERS - 2:
                polar_ref[at, :] = part
            later[at, :] = part.astype(BF16)
        now, later = later, now
    gram_of(now, gram_ref)
    turned = dot(emb_ref[...], now[...], NT)
    out_ref[...] = (1.5 * turned - 0.5 * dot(turned.astype(BF16), gram_ref[...])).astype(BF16)


def finish(side, mine, other, embeddings):
    return pl.pallas_call(
        polar_kernel,
        out_shape=(
            jax.ShapeDtypeStruct((TOK, D), BF16),
            jax.ShapeDtypeStruct((SUBS, DS, K), BF16),
        ),
        in_specs=[SMEM] + [VMEM] * 3,
        out_specs=(VMEM,) * 2,
        scratch_shapes=[
            pltpu.VMEM((D, D), BF16),
            pltpu.VMEM((D, D), BF16),
            pltpu.VMEM((D, D), BF16),
            pltpu.VMEM((D, D), F32),
        ],
        compiler_params=pltpu.CompilerParams(vmem_limit_bytes=32 * MIB),
        cost_estimate=pl.CostEstimate(flops=20 * 10**9, bytes_accessed=8 * 10**6, transcendentals=0),
        name="polar",
    )(side, mine, other, embeddings)


def local(embeddings, rotation, pq_codes, codebook):
    codes = pq_codes.T
    core = lax.axis_index("core")
    mine, other = jnp.full((1,), core, jnp.int32), jnp.full((1,), 1 - core, jnp.int32)

    theirs = lax.dynamic_index_in_dim(codebook, 1 - core, 0, keepdims=False)
    other_book = gather(theirs, ROW, HALF).reshape(HALF * DS, K)
    table = tables(embeddings, rotation, codes)
    mine_book = swap(other_book)
    sent = crosses(other, embeddings, codes, other_book, table)
    sent, mine_book = lax.optimization_barrier((sent, mine_book))
    got = swap(sent)
    kept = crosses(mine, embeddings, codes, mine_book, table)

    pair = (got.astype(F32) + kept.astype(F32)).astype(BF16)
    boxed = spread(pair.reshape(16, 16, WIDE), BOX)
    counted = boxed[:8, BACK:].reshape(2, 2, K)
    counted = counted[:, 0] + LOW * counted[:, 1]
    rest = jnp.floor(counted * (1.0 / LOW))
    high = jnp.floor(rest * (1.0 / LOW))
    digits = jnp.concatenate([counted - LOW * rest, rest - LOW * high, high], axis=0)
    digits = jnp.pad(digits.reshape(12, 128), ((0, 4), (0, 0)))
    packed = jnp.concatenate([boxed[:, :BACK], digits], axis=1).astype(BF16)
    packed = total(packed, "yh", 4).astype(BF16)
    summed = total(packed, "zh", 4)

    counted = summed[:12, BACK:].reshape(3, 2, K)
    counted = counted[0] + LOW * counted[1] + (LOW * LOW) * counted[2]
    box = lax.axis_index(BOX)
    fresh = []
    for half in range(2):
        old = lax.dynamic_slice_in_dim(mine_book, box * DS + MINE * half, DS, 0).astype(F32)
        sums = summed[:, 2 * D + K * half : 2 * D + K * half + K]
        count = counted[half : half + 1]
        fresh.append(jnp.where(count > 0, sums / jnp.maximum(count, 1.0), old))
    own = jnp.concatenate([summed[:, : 2 * D]] + fresh, axis=1).astype(BF16)

    rows = gather(own, BOX, 16).reshape(MINE, BACK)
    rerotated, new_codebook = finish(mine, rows, swap(rows), embeddings)
    return (new_codebook, rerotated)


def solution(mesh):
    split = Mesh(mesh.devices.reshape(4, 2, 2, 4, 4, 2), AXES)
    placed = (P(AXES, None), P(), P(AXES, None), P(ROW, None, None))
    return jax.shard_map(
        local, mesh=split, in_specs=placed, out_specs=(P(), P(AXES, None)), check_vma=False
    )
```

```python
import jax
import jax.numpy as jnp
from jax import lax
from jax.experimental import pallas as pl
from jax.experimental.pallas import tpu as pltpu
from jax.sharding import Mesh, PartitionSpec as P

ITERS = 4
EPSILON = 1e-06
F32 = jnp.float32
BF16 = jnp.bfloat16

AXES = ("yh", "yl", "core", "x", "zh", "zl")
ROW = ("x", "zh", "zl")
BOX = ("x", "yl", "zl")

D = 1024
SUBS = 64
HALF = SUBS // 2
QUARTER = SUBS // 4
DS = 16
K = 256
TOK = 512
MINE = TOK // 2
LOW = 64.0
BACK = 2 * D + 2 * K
WIDE = BACK + 128

NN = (((1,), (0,)), ((), ()))
NT = (((1,), (1,)), ((), ()))
MIB = 1024 * 1024
VMEM = pl.BlockSpec(memory_space=pltpu.VMEM)
SMEM = pl.BlockSpec(memory_space=pltpu.SMEM)


def dot(a, b, dims=NN):
    return lax.dot_general(a, b, dims, preferred_element_type=F32)


def gather(value, axes, peers):
    return lax.all_to_all(
        jnp.broadcast_to(value[None], (peers,) + value.shape), axes, 0, 0, tiled=True
    )


def spread(parts, axes):
    return jnp.sum(lax.all_to_all(parts, axes, 0, 0, tiled=True).astype(F32), axis=0)


def total(value, axes, peers):
    return jnp.sum(gather(value, axes, peers).astype(F32), axis=0)


def swap(value):
    return lax.ppermute(value, "core", [(0, 1), (1, 0)])


def picks(codes_ref, sub):
    row = codes_ref[pl.ds(sub, 1), :].astype(jnp.int16)
    levels = lax.broadcasted_iota(jnp.int32, (K, TOK), 0).astype(jnp.int16)
    return jnp.where(levels == row, jnp.ones((), BF16), jnp.zeros((), BF16))


def tables_kernel(emb_hbm, rot_hbm, codes_hbm, out_ref, emb_ref, rot_ref, codes_ref, sems):
    copies = [
        pltpu.make_async_copy(source, target, sems.at[i])
        for i, (source, target) in enumerate(((emb_hbm, emb_ref), (rot_hbm, rot_ref), (codes_hbm, codes_ref)))
    ]
    for copy in copies:
        copy.start()
    lane = lax.broadcasted_iota(jnp.int32, (K, 128), 1) // DS
    line = lax.broadcasted_iota(jnp.int32, (DS, 128), 0)
    for copy in copies:
        copy.wait()

    rotated = dot(emb_ref[...], rot_ref[...]).astype(BF16)
    ones = jnp.ones((TOK, 128), BF16)

    def group(g):
        right = jnp.concatenate([rotated[:, 128 * g : 128 * g + 128], ones], axis=1)
        sums = jnp.zeros((K, 128), F32)
        counts = jnp.zeros((K, 128), F32)
        for place in range(8):
            both = dot(picks(codes_ref, 8 * g + place), right)
            sums = jnp.where(lane == place, both[:, :128], sums)
            counts = jnp.where(lane == place, both[:, 128:], counts)
        return sums.T, counts.T

    for g in range(4):
        made = [group(g), group(g + 4)]
        for place in range(8):
            here = slice(DS * place, DS * place + DS)
            at = pl.ds((4 * g + place // 2) * DS, DS)
            digits = jnp.zeros((DS, 128), F32)
            for half, (sums, counts) in enumerate(made):
                out_ref[place % 2, at, K * half : K * half + K] = sums[here].astype(BF16)
                count = counts[here]
                high = jnp.floor(count * (1.0 / LOW))
                low = count - LOW * high
                parts = (low[:, :128], low[:, 128:], high[:, :128], high[:, 128:])
                for row, part in enumerate(parts):
                    digits = jnp.where(line == 4 * half + row, part, digits)
            out_ref[place % 2, at, 2 * K :] = digits.astype(BF16)


def tables(embeddings, rotation, codes):
    return pl.pallas_call(
        tables_kernel,
        out_shape=jax.ShapeDtypeStruct((2, MINE, 2 * K + 128), BF16),
        in_specs=[pl.BlockSpec(memory_space=pl.ANY)] * 3,
        out_specs=VMEM,
        scratch_shapes=[
            pltpu.VMEM((TOK, D), BF16),
            pltpu.VMEM((D, D), BF16),
            pltpu.VMEM((SUBS, TOK), jnp.int32),
            pltpu.SemaphoreType.DMA((3,)),
        ],
        compiler_params=pltpu.CompilerParams(vmem_limit_bytes=60 * MIB),
        cost_estimate=pl.CostEstimate(flops=8 * 10**9, bytes_accessed=4 * 10**6, transcendentals=0),
        name="tables",
    )(embeddings, rotation, codes)


def cross_kernel(side_ref, emb_ref, codes_ref, book_ref, table_ref, out_ref, rebuilt_ref):
    side = side_ref[0]

    def step(q, carry):
        at = pl.ds(pl.multiple_of(q * DS, DS), DS)
        rebuilt_ref[at, :] = dot(book_ref[at, :], picks(codes_ref, 2 * q + side)).astype(BF16)
        return carry

    lax.fori_loop(0, HALF, step, 0, unroll=32)
    part = dot(rebuilt_ref[...], emb_ref[...])
    out_ref[:, :D] = part[:MINE].astype(BF16)
    out_ref[:, D : 2 * D] = part[MINE:].astype(BF16)
    out_ref[:, 2 * D :] = table_ref[side]


def crosses(side, embeddings, codes, book, table):
    return pl.pallas_call(
        cross_kernel,
        out_shape=jax.ShapeDtypeStruct((MINE, WIDE), BF16),
        in_specs=[SMEM] + [VMEM] * 4,
        out_specs=VMEM,
        scratch_shapes=[pltpu.VMEM((TOK, TOK), BF16)],
        compiler_params=pltpu.CompilerParams(vmem_limit_bytes=16 * MIB),
        cost_estimate=pl.CostEstimate(flops=4 * 10**9, bytes_accessed=4 * 10**6, transcendentals=0),
        name="crosses",
    )(side, embeddings, codes, book, table)


def gram_of(y_ref, gram_ref, squares=False):
    size = D // 4
    total = 0.0
    for i in range(4):
        at = slice(i * size, (i + 1) * size)
        part = dot(y_ref[at, :], y_ref[i * size :, :], NT)
        gram_ref[at, i * size :] = part.astype(BF16)
        if i < 3:
            gram_ref[(i + 1) * size :, at] = part[:, size:].astype(BF16).T
        if squares:
            total = total + jnp.sum(part[:, :size] * part[:, :size], keepdims=True)
            if i < 3:
                total = total + 2.0 * jnp.sum(part[:, size:] * part[:, size:], keepdims=True)
    return total


def polar_kernel(side_ref, mine_ref, other_ref, emb_ref, out_ref, book_ref, a_ref, b_ref, gram_ref, polar_ref):
    side = side_ref[0]
    for rows_ref, at in ((mine_ref, side), (other_ref, 1 - side)):
        for q in range(HALF):
            here = pl.ds((q % QUARTER) * DS, DS)
            left = (q // QUARTER) * D
            a_ref[pl.ds(pl.multiple_of((2 * q + at) * DS, DS), DS), :] = rows_ref[here, left : left + D]
            left = 2 * D + (q // QUARTER) * K
            book_ref[2 * q + at] = rows_ref[here, left : left + K]

    blocks = [pl.ds(i * (D // 2), D // 2) for i in range(2)]
    norm_square = jnp.sqrt(gram_of(a_ref, gram_ref, squares=True)) + EPSILON
    scale = lax.rsqrt(norm_square)
    for at in blocks:
        moved = dot(gram_ref[at, :], a_ref[...])
        part = (1.5 * scale) * a_ref[at, :].astype(F32) - (0.5 * scale / norm_square) * moved
        polar_ref[at, :] = part
        b_ref[at, :] = part.astype(BF16)
    now, later = b_ref, a_ref
    for turn in range(1, ITERS - 1):
        gram_of(now, gram_ref)
        for at in blocks:
            part = 1.5 * polar_ref[at, :] - 0.5 * dot(gram_ref[at, :], now[...])
            if turn < ITERS - 2:
                polar_ref[at, :] = part
            later[at, :] = part.astype(BF16)
        now, later = later, now
    gram_of(now, gram_ref)
    turned = dot(emb_ref[...], now[...], NT)
    out_ref[...] = (1.5 * turned - 0.5 * dot(turned.astype(BF16), gram_ref[...])).astype(BF16)


def finish(side, mine, other, embeddings):
    return pl.pallas_call(
        polar_kernel,
        out_shape=(
            jax.ShapeDtypeStruct((TOK, D), BF16),
            jax.ShapeDtypeStruct((SUBS, DS, K), BF16),
        ),
        in_specs=[SMEM] + [VMEM] * 3,
        out_specs=(VMEM,) * 2,
        scratch_shapes=[
            pltpu.VMEM((D, D), BF16),
            pltpu.VMEM((D, D), BF16),
            pltpu.VMEM((D, D), BF16),
            pltpu.VMEM((D, D), F32),
        ],
        compiler_params=pltpu.CompilerParams(vmem_limit_bytes=32 * MIB),
        cost_estimate=pl.CostEstimate(flops=20 * 10**9, bytes_accessed=8 * 10**6, transcendentals=0),
        name="polar",
    )(side, mine, other, embeddings)


def local(embeddings, rotation, pq_codes, codebook):
    codes = pq_codes.T
    core = lax.axis_index("core")
    mine, other = jnp.full((1,), core, jnp.int32), jnp.full((1,), 1 - core, jnp.int32)

    theirs = lax.dynamic_index_in_dim(codebook, 1 - core, 0, keepdims=False)
    other_book = gather(theirs, ROW, HALF).reshape(HALF * DS, K)
    table = tables(embeddings, rotation, codes)
    mine_book = swap(other_book)
    sent = crosses(other, embeddings, codes, other_book, table)
    sent, mine_book = lax.optimization_barrier((sent, mine_book))
    got = swap(sent)
    kept = crosses(mine, embeddings, codes, mine_book, table)

    pair = (got.astype(F32) + kept.astype(F32)).astype(BF16)
    boxed = spread(pair.reshape(16, 16, WIDE), BOX)
    counted = boxed[:8, BACK:].reshape(2, 2, K)
    counted = counted[:, 0] + LOW * counted[:, 1]
    rest = jnp.floor(counted * (1.0 / LOW))
    high = jnp.floor(rest * (1.0 / LOW))
    digits = jnp.concatenate([counted - LOW * rest, rest - LOW * high, high], axis=0)
    digits = jnp.pad(digits.reshape(12, 128), ((0, 4), (0, 0)))
    packed = jnp.concatenate([boxed[:, :BACK], digits], axis=1).astype(BF16)
    packed = total(packed, "yh", 4).astype(BF16)
    summed = total(packed, "zh", 4)

    counted = summed[:12, BACK:].reshape(3, 2, K)
    counted = counted[0] + LOW * counted[1] + (LOW * LOW) * counted[2]
    box = lax.axis_index(BOX)
    fresh = []
    for half in range(2):
        old = lax.dynamic_slice_in_dim(mine_book, box * DS + MINE * half, DS, 0).astype(F32)
        sums = summed[:, 2 * D + K * half : 2 * D + K * half + K]
        count = counted[half : half + 1]
        fresh.append(jnp.where(count > 0, sums / jnp.maximum(count, 1.0), old))
    own = jnp.concatenate([summed[:, : 2 * D]] + fresh, axis=1).astype(BF16)

    rows = gather(own, BOX, 16).reshape(MINE, BACK)
    rerotated, new_codebook = finish(mine, rows, swap(rows), embeddings)
    return (new_codebook, rerotated)


def solution(mesh):
    split = Mesh(mesh.devices.reshape(4, 2, 2, 4, 4, 2), AXES)
    placed = (P(AXES, None), P(), P(AXES, None), P(ROW, None, None))
    return jax.shard_map(
        local, mesh=split, in_specs=placed, out_specs=(P(), P(AXES, None)), check_vma=False
    )
```

```python
import jax
import jax.numpy as jnp
from jax import lax
from jax.experimental import pallas as pl
from jax.experimental.pallas import tpu as pltpu
from jax.sharding import Mesh, PartitionSpec as P

EPSILON = 1e-06
F32 = jnp.float32
BF16 = jnp.bfloat16

AXES = ("yh", "yl", "core", "x", "zh", "zl")
ROW = ("x", "zh", "zl")
BOX = ("x", "yl", "zl")

D = 1024
SUBS = 64
HALF = SUBS // 2
QUARTER = SUBS // 4
DS = 16
K = 256
TOK = 512
MINE = TOK // 2
LOW = 64.0
BACK = 2 * D + 2 * K
WIDE = BACK + 128

NN = (((1,), (0,)), ((), ()))
NT = (((1,), (1,)), ((), ()))
MIB = 1024 * 1024
VMEM = pl.BlockSpec(memory_space=pltpu.VMEM)
SMEM = pl.BlockSpec(memory_space=pltpu.SMEM)


def dot(a, b, dims=NN):
    return lax.dot_general(a, b, dims, preferred_element_type=F32)


def gather(value, axes, peers):
    return lax.all_to_all(
        jnp.broadcast_to(value[None], (peers,) + value.shape), axes, 0, 0, tiled=True
    )


def spread(parts, axes):
    return jnp.sum(lax.all_to_all(parts, axes, 0, 0, tiled=True).astype(F32), axis=0)


def total(value, axes, peers):
    return jnp.sum(gather(value, axes, peers).astype(F32), axis=0)


def swap(value):
    return lax.ppermute(value, "core", [(0, 1), (1, 0)])


def picks(codes_ref, sub):
    row = codes_ref[pl.ds(sub, 1), :].astype(jnp.int16)
    levels = lax.broadcasted_iota(jnp.int32, (K, TOK), 0).astype(jnp.int16)
    return jnp.where(levels == row, jnp.ones((), BF16), jnp.zeros((), BF16))


def tables_kernel(emb_hbm, rot_hbm, codes_hbm, out_ref, emb_ref, rot_ref, codes_ref, sems):
    copies = [
        pltpu.make_async_copy(source, target, sems.at[i])
        for i, (source, target) in enumerate(((emb_hbm, emb_ref), (rot_hbm, rot_ref), (codes_hbm, codes_ref)))
    ]
    for copy in copies:
        copy.start()
    lane = lax.broadcasted_iota(jnp.int32, (K, 128), 1) // DS
    line = lax.broadcasted_iota(jnp.int32, (DS, 128), 0)
    for copy in copies:
        copy.wait()

    rotated = dot(emb_ref[...], rot_ref[...]).astype(BF16)
    ones = jnp.ones((TOK, 128), BF16)

    def group(g):
        right = jnp.concatenate([rotated[:, 128 * g : 128 * g + 128], ones], axis=1)
        sums = jnp.zeros((K, 128), F32)
        counts = jnp.zeros((K, 128), F32)
        for place in range(8):
            both = dot(picks(codes_ref, 8 * g + place), right)
            sums = jnp.where(lane == place, both[:, :128], sums)
            counts = jnp.where(lane == place, both[:, 128:], counts)
        return sums.T, counts.T

    for g in range(4):
        made = [group(g), group(g + 4)]
        for place in range(8):
            here = slice(DS * place, DS * place + DS)
            at = pl.ds((4 * g + place // 2) * DS, DS)
            digits = jnp.zeros((DS, 128), F32)
            for half, (sums, counts) in enumerate(made):
                out_ref[place % 2, at, K * half : K * half + K] = sums[here].astype(BF16)
                count = counts[here]
                high = jnp.floor(count * (1.0 / LOW))
                low = count - LOW * high
                parts = (low[:, :128], low[:, 128:], high[:, :128], high[:, 128:])
                for row, part in enumerate(parts):
                    digits = jnp.where(line == 4 * half + row, part, digits)
            out_ref[place % 2, at, 2 * K :] = digits.astype(BF16)


def tables(embeddings, rotation, codes):
    return pl.pallas_call(
        tables_kernel,
        out_shape=jax.ShapeDtypeStruct((2, MINE, 2 * K + 128), BF16),
        in_specs=[pl.BlockSpec(memory_space=pl.ANY)] * 3,
        out_specs=VMEM,
        scratch_shapes=[
            pltpu.VMEM((TOK, D), BF16),
            pltpu.VMEM((D, D), BF16),
            pltpu.VMEM((SUBS, TOK), jnp.int32),
            pltpu.SemaphoreType.DMA((3,)),
        ],
        compiler_params=pltpu.CompilerParams(vmem_limit_bytes=60 * MIB),
        cost_estimate=pl.CostEstimate(flops=8 * 10**9, bytes_accessed=4 * 10**6, transcendentals=0),
        name="tables",
    )(embeddings, rotation, codes)


def cross_kernel(side_ref, emb_ref, codes_ref, book_ref, table_ref, out_ref, rebuilt_ref):
    side = side_ref[0]

    def step(q, carry):
        at = pl.ds(pl.multiple_of(q * DS, DS), DS)
        rebuilt_ref[at, :] = dot(book_ref[at, :], picks(codes_ref, 2 * q + side)).astype(BF16)
        return carry

    lax.fori_loop(0, HALF, step, 0, unroll=32)
    part = dot(rebuilt_ref[...], emb_ref[...])
    out_ref[:, :D] = part[:MINE].astype(BF16)
    out_ref[:, D : 2 * D] = part[MINE:].astype(BF16)
    out_ref[:, 2 * D :] = table_ref[side]


def crosses(side, embeddings, codes, book, table):
    return pl.pallas_call(
        cross_kernel,
        out_shape=jax.ShapeDtypeStruct((MINE, WIDE), BF16),
        in_specs=[SMEM] + [VMEM] * 4,
        out_specs=VMEM,
        scratch_shapes=[pltpu.VMEM((TOK, TOK), BF16)],
        compiler_params=pltpu.CompilerParams(vmem_limit_bytes=16 * MIB),
        cost_estimate=pl.CostEstimate(flops=4 * 10**9, bytes_accessed=4 * 10**6, transcendentals=0),
        name="crosses",
    )(side, embeddings, codes, book, table)


PARTS = 4
PART = D // PARTS


def symmetric(product, store):
    for i in range(PARTS):
        at, right = slice(i * PART, (i + 1) * PART), slice(i * PART, D)
        for target, value in store(at, right, product(at, right)):
            target[at, right] = value
            if i < PARTS - 1:
                target[(i + 1) * PART :, at] = value[:, PART:].T


def two_steps(g_ref, g2_ref, k_ref, w_ref):
    def square(at, right, part):
        k = 0.0625 * part - 0.5625 * g_ref[at, right].astype(F32)
        return (g2_ref, part.astype(BF16)), (k_ref, k.astype(BF16))

    symmetric(lambda at, right: dot(g_ref[at, :], g_ref[:, right]), square)

    def rest(at, right, part):
        w = part + 1.6875 * g2_ref[at, right].astype(F32) - 2.4375 * g_ref[at, right].astype(F32)
        return ((w_ref, w.astype(BF16)),)

    symmetric(lambda at, right: dot(g2_ref[at, :], k_ref[:, right]), rest)


def polar_kernel(side_ref, mine_ref, other_ref, emb_ref, out_ref, book_ref, y_ref, z_ref, g_ref, g2_ref, k_ref, w_ref, full_ref):
    side = side_ref[0]
    for rows_ref, at in ((mine_ref, side), (other_ref, 1 - side)):
        for q in range(HALF):
            here = pl.ds((q % QUARTER) * DS, DS)
            left = (q // QUARTER) * D
            y_ref[pl.ds(pl.multiple_of((2 * q + at) * DS, DS), DS), :] = rows_ref[here, left : left + D]
            left = 2 * D + (q // QUARTER) * K
            book_ref[2 * q + at] = rows_ref[here, left : left + K]

    squares = 0.0
    for i in range(PARTS):
        at, right = slice(i * PART, (i + 1) * PART), slice(i * PART, D)
        part = dot(y_ref[at, :], y_ref[right, :], NT)
        full_ref[at, right] = part
        squares = squares + jnp.sum(part[:, :PART] * part[:, :PART], keepdims=True)
        if i < PARTS - 1:
            squares = squares + 2.0 * jnp.sum(part[:, PART:] * part[:, PART:], keepdims=True)
    norm_square = jnp.sqrt(squares) + EPSILON
    scale = lax.rsqrt(norm_square)
    shrink = 1.0 / norm_square

    symmetric(
        lambda at, right: full_ref[at, right],
        lambda at, right, part: ((g_ref, (part * shrink).astype(BF16)),),
    )
    two_steps(g_ref, g2_ref, k_ref, w_ref)
    for i in range(2):
        at = slice(i * (D // 2), (i + 1) * (D // 2))
        part = 2.25 * y_ref[at, :].astype(F32) + dot(w_ref[at, :], y_ref[...])
        z_ref[at, :] = (scale * part).astype(BF16)

    symmetric(
        lambda at, right: dot(z_ref[at, :], z_ref[right, :], NT),
        lambda at, right, part: ((g_ref, part.astype(BF16)),),
    )
    turned = dot(emb_ref[...], z_ref[...], NT)
    two_steps(g_ref, g2_ref, k_ref, w_ref)
    out_ref[...] = (2.25 * turned + dot(turned.astype(BF16), w_ref[...])).astype(BF16)


def finish(side, mine, other, embeddings):
    return pl.pallas_call(
        polar_kernel,
        out_shape=(
            jax.ShapeDtypeStruct((TOK, D), BF16),
            jax.ShapeDtypeStruct((SUBS, DS, K), BF16),
        ),
        in_specs=[SMEM] + [VMEM] * 3,
        out_specs=(VMEM,) * 2,
        scratch_shapes=[
            pltpu.VMEM((D, D), BF16),
            pltpu.VMEM((D, D), BF16),
            pltpu.VMEM((D, D), BF16),
            pltpu.VMEM((D, D), BF16),
            pltpu.VMEM((D, D), BF16),
            pltpu.VMEM((D, D), BF16),
            pltpu.VMEM((D, D), F32),
        ],
        compiler_params=pltpu.CompilerParams(vmem_limit_bytes=32 * MIB),
        cost_estimate=pl.CostEstimate(flops=20 * 10**9, bytes_accessed=8 * 10**6, transcendentals=0),
        name="polar",
    )(side, mine, other, embeddings)


def local(embeddings, rotation, pq_codes, codebook):
    codes = pq_codes.T
    core = lax.axis_index("core")
    mine, other = jnp.full((1,), core, jnp.int32), jnp.full((1,), 1 - core, jnp.int32)

    theirs = lax.dynamic_index_in_dim(codebook, 1 - core, 0, keepdims=False)
    other_book = gather(theirs, ROW, HALF).reshape(HALF * DS, K)
    table = tables(embeddings, rotation, codes)
    mine_book = swap(other_book)
    sent = crosses(other, embeddings, codes, other_book, table)
    sent, mine_book = lax.optimization_barrier((sent, mine_book))
    got = swap(sent)
    kept = crosses(mine, embeddings, codes, mine_book, table)

    pair = (got.astype(F32) + kept.astype(F32)).astype(BF16)
    boxed = spread(pair.reshape(16, 16, WIDE), BOX)
    counted = boxed[:8, BACK:].reshape(2, 2, K)
    counted = counted[:, 0] + LOW * counted[:, 1]
    rest = jnp.floor(counted * (1.0 / LOW))
    high = jnp.floor(rest * (1.0 / LOW))
    digits = jnp.concatenate([counted - LOW * rest, rest - LOW * high, high], axis=0)
    digits = jnp.pad(digits.reshape(12, 128), ((0, 4), (0, 0)))
    packed = jnp.concatenate([boxed[:, :BACK], digits], axis=1).astype(BF16)
    packed = total(packed, "yh", 4).astype(BF16)
    summed = total(packed, "zh", 4)
    summed, mine_book = lax.optimization_barrier((summed, mine_book))

    counted = summed[:12, BACK:].reshape(3, 2, K)
    counted = counted[0] + LOW * counted[1] + (LOW * LOW) * counted[2]
    box = lax.axis_index(BOX)
    fresh = []
    for half in range(2):
        old = lax.dynamic_slice_in_dim(mine_book, box * DS + MINE * half, DS, 0).astype(F32)
        sums = summed[:, 2 * D + K * half : 2 * D + K * half + K]
        count = counted[half : half + 1]
        fresh.append(jnp.where(count > 0, sums / jnp.maximum(count, 1.0), old))
    own = jnp.concatenate([summed[:, : 2 * D]] + fresh, axis=1).astype(BF16)

    rows = gather(own, BOX, 16).reshape(MINE, BACK)
    rerotated, new_codebook = finish(mine, rows, swap(rows), embeddings)
    return (new_codebook, rerotated)


def solution(mesh):
    split = Mesh(mesh.devices.reshape(4, 2, 2, 4, 4, 2), AXES)
    placed = (P(AXES, None), P(), P(AXES, None), P(ROW, None, None))
    return jax.shard_map(
        local, mesh=split, in_specs=placed, out_specs=(P(), P(AXES, None)), check_vma=False
    )
```

```python
import jax
import jax.numpy as jnp
from jax import lax
from jax.experimental import pallas as pl
from jax.experimental.pallas import tpu as pltpu
from jax.sharding import Mesh, PartitionSpec as P

EPSILON = 1e-06
F32 = jnp.float32
BF16 = jnp.bfloat16

AXES = ("yh", "yl", "core", "x", "zh", "zl")
ROW = ("x", "zh", "zl")
BOX = ("x", "yl", "zl")

D = 1024
SUBS = 64
HALF = SUBS // 2
QUARTER = SUBS // 4
DS = 16
K = 256
TOK = 512
MINE = TOK // 2
LOW = 64.0
BACK = 2 * D + 2 * K
WIDE = BACK + 128

NN = (((1,), (0,)), ((), ()))
NT = (((1,), (1,)), ((), ()))
MIB = 1024 * 1024
VMEM = pl.BlockSpec(memory_space=pltpu.VMEM)
SMEM = pl.BlockSpec(memory_space=pltpu.SMEM)


def dot(a, b, dims=NN):
    return lax.dot_general(a, b, dims, preferred_element_type=F32)


def far_groups(turn):
    groups = []
    for yl in range(2):
        for core in range(2):
            for x in range(4):
                for other in range(4):
                    for zl in range(2):
                        along_y = core == turn
                        places = [(i, other) if along_y else (other, i) for i in range(4)]
                        groups.append(
                            [((((yh * 2 + yl) * 2 + core) * 4 + x) * 4 + zh) * 2 + zl for yh, zh in places]
                        )
    return groups


def gather(value, axes, peers, groups=None):
    spreadout = jnp.broadcast_to(value[None], (peers,) + value.shape)
    return lax.all_to_all(spreadout, axes, 0, 0, axis_index_groups=groups, tiled=True)


def spread(parts, axes):
    return jnp.sum(lax.all_to_all(parts, axes, 0, 0, tiled=True).astype(F32), axis=0)


def total(value, turn):
    return jnp.sum(gather(value, AXES, 4, far_groups(turn)).astype(F32), axis=0)


def swap(value):
    return lax.ppermute(value, "core", [(0, 1), (1, 0)])


def picks(codes_ref, sub):
    row = codes_ref[pl.ds(sub, 1), :].astype(jnp.int16)
    levels = lax.broadcasted_iota(jnp.int32, (K, TOK), 0).astype(jnp.int16)
    return jnp.where(levels == row, jnp.ones((), BF16), jnp.zeros((), BF16))


def tables_kernel(emb_hbm, rot_hbm, codes_hbm, out_ref, emb_ref, rot_ref, codes_ref, sems):
    copies = [
        pltpu.make_async_copy(source, target, sems.at[i])
        for i, (source, target) in enumerate(((emb_hbm, emb_ref), (rot_hbm, rot_ref), (codes_hbm, codes_ref)))
    ]
    for copy in copies:
        copy.start()
    lane = lax.broadcasted_iota(jnp.int32, (K, 128), 1) // DS
    line = lax.broadcasted_iota(jnp.int32, (DS, 128), 0)
    for copy in copies:
        copy.wait()

    rotated = dot(emb_ref[...], rot_ref[...]).astype(BF16)
    ones = jnp.ones((TOK, 128), BF16)

    def group(g):
        right = jnp.concatenate([rotated[:, 128 * g : 128 * g + 128], ones], axis=1)
        sums = jnp.zeros((K, 128), F32)
        counts = jnp.zeros((K, 128), F32)
        for place in range(8):
            both = dot(picks(codes_ref, 8 * g + place), right)
            sums = jnp.where(lane == place, both[:, :128], sums)
            counts = jnp.where(lane == place, both[:, 128:], counts)
        return sums.T, counts.T

    for g in range(4):
        made = [group(g), group(g + 4)]
        for place in range(8):
            here = slice(DS * place, DS * place + DS)
            at = pl.ds((4 * g + place // 2) * DS, DS)
            digits = jnp.zeros((DS, 128), F32)
            for half, (sums, counts) in enumerate(made):
                out_ref[place % 2, at, K * half : K * half + K] = sums[here].astype(BF16)
                count = counts[here]
                high = jnp.floor(count * (1.0 / LOW))
                low = count - LOW * high
                parts = (low[:, :128], low[:, 128:], high[:, :128], high[:, 128:])
                for row, part in enumerate(parts):
                    digits = jnp.where(line == 4 * half + row, part, digits)
            out_ref[place % 2, at, 2 * K :] = digits.astype(BF16)


def tables(embeddings, rotation, codes):
    return pl.pallas_call(
        tables_kernel,
        out_shape=jax.ShapeDtypeStruct((2, MINE, 2 * K + 128), BF16),
        in_specs=[pl.BlockSpec(memory_space=pl.ANY)] * 3,
        out_specs=VMEM,
        scratch_shapes=[
            pltpu.VMEM((TOK, D), BF16),
            pltpu.VMEM((D, D), BF16),
            pltpu.VMEM((SUBS, TOK), jnp.int32),
            pltpu.SemaphoreType.DMA((3,)),
        ],
        compiler_params=pltpu.CompilerParams(vmem_limit_bytes=53 * MIB),
        cost_estimate=pl.CostEstimate(flops=8 * 10**9, bytes_accessed=4 * 10**6, transcendentals=0),
        name="tables",
    )(embeddings, rotation, codes)


def cross_kernel(side_ref, emb_ref, codes_ref, book_ref, table_ref, out_ref, rebuilt_ref):
    side = side_ref[0]

    def step(q, carry):
        at = pl.ds(pl.multiple_of(q * DS, DS), DS)
        rebuilt_ref[at, :] = dot(book_ref[at, :], picks(codes_ref, 2 * q + side)).astype(BF16)
        return carry

    lax.fori_loop(0, HALF, step, 0, unroll=32)
    part = dot(rebuilt_ref[...], emb_ref[...])
    out_ref[:, :D] = part[:MINE].astype(BF16)
    out_ref[:, D : 2 * D] = part[MINE:].astype(BF16)
    out_ref[:, 2 * D :] = table_ref[side]


def crosses(side, embeddings, codes, book, table):
    return pl.pallas_call(
        cross_kernel,
        out_shape=jax.ShapeDtypeStruct((MINE, WIDE), BF16),
        in_specs=[SMEM] + [VMEM] * 4,
        out_specs=VMEM,
        scratch_shapes=[pltpu.VMEM((TOK, TOK), BF16)],
        compiler_params=pltpu.CompilerParams(vmem_limit_bytes=16 * MIB),
        cost_estimate=pl.CostEstimate(flops=4 * 10**9, bytes_accessed=4 * 10**6, transcendentals=0),
        name="crosses",
    )(side, embeddings, codes, book, table)


PARTS = 4
PART = D // PARTS


def symmetric(product, store):
    for i in range(PARTS):
        at, right = slice(i * PART, (i + 1) * PART), slice(i * PART, D)
        for target, value in store(at, right, product(at, right)):
            target[at, right] = value
            if i < PARTS - 1:
                target[(i + 1) * PART :, at] = value[:, PART:].T


def two_steps(g_ref, g2_ref, k_ref, w_ref):
    def square(at, right, part):
        k = 0.0625 * part - 0.5625 * g_ref[at, right].astype(F32)
        return (g2_ref, part.astype(BF16)), (k_ref, k.astype(BF16))

    symmetric(lambda at, right: dot(g_ref[at, :], g_ref[:, right]), square)

    def rest(at, right, part):
        w = part + 1.6875 * g2_ref[at, right].astype(F32) - 2.4375 * g_ref[at, right].astype(F32)
        return ((w_ref, w.astype(BF16)),)

    symmetric(lambda at, right: dot(g2_ref[at, :], k_ref[:, right]), rest)


def polar_kernel(side_ref, mine_ref, other_ref, emb_ref, out_ref, book_ref, y_ref, z_ref, g_ref, g2_ref, k_ref, w_ref, full_ref):
    side = side_ref[0]
    for rows_ref, at in ((mine_ref, side), (other_ref, 1 - side)):
        for q in range(HALF):
            here = pl.ds((q % QUARTER) * DS, DS)
            left = (q // QUARTER) * D
            y_ref[pl.ds(pl.multiple_of((2 * q + at) * DS, DS), DS), :] = rows_ref[here, left : left + D]
            left = 2 * D + (q // QUARTER) * K
            book_ref[2 * q + at] = rows_ref[here, left : left + K]

    squares = 0.0
    for i in range(PARTS):
        at, right = slice(i * PART, (i + 1) * PART), slice(i * PART, D)
        part = dot(y_ref[at, :], y_ref[right, :], NT)
        full_ref[at, right] = part
        squares = squares + jnp.sum(part[:, :PART] * part[:, :PART], keepdims=True)
        if i < PARTS - 1:
            squares = squares + 2.0 * jnp.sum(part[:, PART:] * part[:, PART:], keepdims=True)
    norm_square = jnp.sqrt(squares) + EPSILON
    scale = lax.rsqrt(norm_square)
    shrink = 1.0 / norm_square

    symmetric(
        lambda at, right: full_ref[at, right],
        lambda at, right, part: ((g_ref, (part * shrink).astype(BF16)),),
    )
    two_steps(g_ref, g2_ref, k_ref, w_ref)
    for i in range(2):
        at = slice(i * (D // 2), (i + 1) * (D // 2))
        part = 2.25 * y_ref[at, :].astype(F32) + dot(w_ref[at, :], y_ref[...])
        z_ref[at, :] = (scale * part).astype(BF16)

    symmetric(
        lambda at, right: dot(z_ref[at, :], z_ref[right, :], NT),
        lambda at, right, part: ((g_ref, part.astype(BF16)),),
    )
    turned = dot(emb_ref[...], z_ref[...], NT)
    two_steps(g_ref, g2_ref, k_ref, w_ref)
    out_ref[...] = (2.25 * turned + dot(turned.astype(BF16), w_ref[...])).astype(BF16)


def finish(side, mine, other, embeddings):
    return pl.pallas_call(
        polar_kernel,
        out_shape=(
            jax.ShapeDtypeStruct((TOK, D), BF16),
            jax.ShapeDtypeStruct((SUBS, DS, K), BF16),
        ),
        in_specs=[SMEM] + [VMEM] * 3,
        out_specs=(VMEM,) * 2,
        scratch_shapes=[
            pltpu.VMEM((D, D), BF16),
            pltpu.VMEM((D, D), BF16),
            pltpu.VMEM((D, D), BF16),
            pltpu.VMEM((D, D), BF16),
            pltpu.VMEM((D, D), BF16),
            pltpu.VMEM((D, D), BF16),
            pltpu.VMEM((D, D), F32),
        ],
        compiler_params=pltpu.CompilerParams(vmem_limit_bytes=32 * MIB),
        cost_estimate=pl.CostEstimate(flops=20 * 10**9, bytes_accessed=8 * 10**6, transcendentals=0),
        name="polar",
    )(side, mine, other, embeddings)


def local(embeddings, rotation, pq_codes, codebook):
    codes = pq_codes.T
    core = lax.axis_index("core")
    mine, other = jnp.full((1,), core, jnp.int32), jnp.full((1,), 1 - core, jnp.int32)

    theirs = lax.dynamic_index_in_dim(codebook, 1 - core, 0, keepdims=False)
    other_book = gather(theirs, ROW, HALF).reshape(HALF * DS, K)
    table = tables(embeddings, rotation, codes)
    mine_book = swap(other_book)
    sent = crosses(other, embeddings, codes, other_book, table)
    sent, mine_book = lax.optimization_barrier((sent, mine_book))
    got = swap(sent)
    kept = crosses(mine, embeddings, codes, mine_book, table)

    pair = (got.astype(F32) + kept.astype(F32)).astype(BF16)
    boxed = spread(pair.reshape(16, 16, WIDE), BOX)
    counted = boxed[:8, BACK:].reshape(2, 2, K)
    counted = counted[:, 0] + LOW * counted[:, 1]
    rest = jnp.floor(counted * (1.0 / LOW))
    high = jnp.floor(rest * (1.0 / LOW))
    digits = jnp.concatenate([counted - LOW * rest, rest - LOW * high, high], axis=0)
    digits = jnp.pad(digits.reshape(12, 128), ((0, 4), (0, 0)))
    packed = jnp.concatenate([boxed[:, :BACK], digits], axis=1).astype(BF16)
    packed = total(packed, 0).astype(BF16)
    packed, box = lax.optimization_barrier((packed, lax.axis_index(BOX)))
    summed = total(packed, 1)
    summed, mine_book, box = lax.optimization_barrier((summed, mine_book, box))

    counted = summed[:12, BACK:].reshape(3, 2, K)
    counted = counted[0] + LOW * counted[1] + (LOW * LOW) * counted[2]
    fresh = []
    for half in range(2):
        old = lax.dynamic_slice_in_dim(mine_book, box * DS + MINE * half, DS, 0).astype(F32)
        sums = summed[:, 2 * D + K * half : 2 * D + K * half + K]
        count = counted[half : half + 1]
        fresh.append(jnp.where(count > 0, sums / jnp.maximum(count, 1.0), old))
    own = jnp.concatenate([summed[:, : 2 * D]] + fresh, axis=1).astype(BF16)

    rows = gather(own, BOX, 16).reshape(MINE, BACK)
    rerotated, new_codebook = finish(mine, rows, swap(rows), embeddings)
    return (new_codebook, rerotated)


def solution(mesh):
    split = Mesh(mesh.devices.reshape(4, 2, 2, 4, 4, 2), AXES)
    placed = (P(AXES, None), P(), P(AXES, None), P(ROW, None, None))
    return jax.shard_map(
        local, mesh=split, in_specs=placed, out_specs=(P(), P(AXES, None)), check_vma=False
    )
```

```python
import jax
import jax.numpy as jnp
from jax import lax
from jax.experimental import pallas as pl
from jax.experimental.pallas import tpu as pltpu
from jax.sharding import Mesh, PartitionSpec as P

EPSILON = 1e-06
F32 = jnp.float32
BF16 = jnp.bfloat16

AXES = ("yh", "yl", "core", "x", "zh", "zl")
ROW = ("x", "zh", "zl")
BOX = ("x", "yl", "zl")

D = 1024
SUBS = 64
HALF = SUBS // 2
QUARTER = SUBS // 4
DS = 16
K = 256
TOK = 512
MINE = TOK // 2
LOW = 64.0
BACK = 2 * D + 2 * K
WIDE = BACK + 128

NN = (((1,), (0,)), ((), ()))
NT = (((1,), (1,)), ((), ()))
MIB = 1024 * 1024
VMEM = pl.BlockSpec(memory_space=pltpu.VMEM)
SMEM = pl.BlockSpec(memory_space=pltpu.SMEM)


def dot(a, b, dims=NN):
    return lax.dot_general(a, b, dims, preferred_element_type=F32)


def far_groups(turn):
    groups = []
    for yl in range(2):
        for core in range(2):
            for x in range(4):
                for other in range(4):
                    for zl in range(2):
                        along_y = core == turn
                        places = [(i, other) if along_y else (other, i) for i in range(4)]
                        groups.append(
                            [((((yh * 2 + yl) * 2 + core) * 4 + x) * 4 + zh) * 2 + zl for yh, zh in places]
                        )
    return groups


def gather(value, axes, peers, groups=None):
    spreadout = jnp.broadcast_to(value[None], (peers,) + value.shape)
    return lax.all_to_all(spreadout, axes, 0, 0, axis_index_groups=groups, tiled=True)


def spread(parts, axes):
    return jnp.sum(lax.all_to_all(parts, axes, 0, 0, tiled=True).astype(F32), axis=0)


def total(value, turn):
    return jnp.sum(gather(value, AXES, 4, far_groups(turn)).astype(F32), axis=0)


def swap(value):
    return lax.ppermute(value, "core", [(0, 1), (1, 0)])


def picks(codes_ref, sub):
    row = codes_ref[pl.ds(sub, 1), :].astype(jnp.int16)
    levels = lax.broadcasted_iota(jnp.int32, (K, TOK), 0).astype(jnp.int16)
    return jnp.where(levels == row, jnp.ones((), BF16), jnp.zeros((), BF16))


def tables_kernel(emb_hbm, rot_hbm, codes_hbm, out_ref, emb_ref, rot_ref, codes_ref, sems):
    copies = [
        pltpu.make_async_copy(source, target, sems.at[i])
        for i, (source, target) in enumerate(((emb_hbm, emb_ref), (rot_hbm, rot_ref), (codes_hbm, codes_ref)))
    ]
    for copy in copies:
        copy.start()
    lane = lax.broadcasted_iota(jnp.int32, (K, 128), 1) // DS
    line = lax.broadcasted_iota(jnp.int32, (DS, 128), 0)
    for copy in copies:
        copy.wait()

    rotated = dot(emb_ref[...], rot_ref[...]).astype(BF16)
    ones = jnp.ones((TOK, 128), BF16)

    def group(g):
        right = jnp.concatenate([rotated[:, 128 * g : 128 * g + 128], ones], axis=1)
        sums = jnp.zeros((K, 128), F32)
        counts = jnp.zeros((K, 128), F32)
        for place in range(8):
            both = dot(picks(codes_ref, 8 * g + place), right)
            sums = jnp.where(lane == place, both[:, :128], sums)
            counts = jnp.where(lane == place, both[:, 128:], counts)
        return sums.T, counts.T

    for g in range(4):
        made = [group(g), group(g + 4)]
        for place in range(8):
            here = slice(DS * place, DS * place + DS)
            at = pl.ds((4 * g + place // 2) * DS, DS)
            digits = jnp.zeros((DS, 128), F32)
            for half, (sums, counts) in enumerate(made):
                out_ref[place % 2, at, K * half : K * half + K] = sums[here].astype(BF16)
                count = counts[here]
                high = jnp.floor(count * (1.0 / LOW))
                low = count - LOW * high
                parts = (low[:, :128], low[:, 128:], high[:, :128], high[:, 128:])
                for row, part in enumerate(parts):
                    digits = jnp.where(line == 4 * half + row, part, digits)
            out_ref[place % 2, at, 2 * K :] = digits.astype(BF16)


def tables(embeddings, rotation, codes):
    return pl.pallas_call(
        tables_kernel,
        out_shape=jax.ShapeDtypeStruct((2, MINE, 2 * K + 128), BF16),
        in_specs=[pl.BlockSpec(memory_space=pl.ANY)] * 3,
        out_specs=VMEM,
        scratch_shapes=[
            pltpu.VMEM((TOK, D), BF16),
            pltpu.VMEM((D, D), BF16),
            pltpu.VMEM((SUBS, TOK), jnp.int32),
            pltpu.SemaphoreType.DMA((3,)),
        ],
        compiler_params=pltpu.CompilerParams(vmem_limit_bytes=53 * MIB),
        cost_estimate=pl.CostEstimate(flops=8 * 10**9, bytes_accessed=4 * 10**6, transcendentals=0),
        name="tables",
    )(embeddings, rotation, codes)


def cross_kernel(side_ref, emb_ref, codes_ref, book_ref, table_ref, out_ref, rebuilt_ref):
    side = side_ref[0]

    def step(q, carry):
        at = pl.ds(pl.multiple_of(q * DS, DS), DS)
        rebuilt_ref[at, :] = dot(book_ref[at, :], picks(codes_ref, 2 * q + side)).astype(BF16)
        return carry

    lax.fori_loop(0, HALF, step, 0, unroll=32)
    part = dot(rebuilt_ref[...], emb_ref[...])
    out_ref[:, :D] = part[:MINE].astype(BF16)
    out_ref[:, D : 2 * D] = part[MINE:].astype(BF16)
    out_ref[:, 2 * D :] = table_ref[side]


def crosses(side, embeddings, codes, book, table):
    return pl.pallas_call(
        cross_kernel,
        out_shape=jax.ShapeDtypeStruct((MINE, WIDE), BF16),
        in_specs=[SMEM] + [VMEM] * 4,
        out_specs=VMEM,
        scratch_shapes=[pltpu.VMEM((TOK, TOK), BF16)],
        compiler_params=pltpu.CompilerParams(vmem_limit_bytes=16 * MIB),
        cost_estimate=pl.CostEstimate(flops=4 * 10**9, bytes_accessed=4 * 10**6, transcendentals=0),
        name="crosses",
    )(side, embeddings, codes, book, table)


PARTS = 4
PART = D // PARTS


def symmetric(product, store):
    for i in range(PARTS):
        at, right = slice(i * PART, (i + 1) * PART), slice(i * PART, D)
        for target, value in store(at, right, product(at, right)):
            target[at, right] = value
            if i < PARTS - 1:
                target[(i + 1) * PART :, at] = value[:, PART:].T


def two_steps(g_ref, g2_ref, k_ref, w_ref):
    def square(at, right, part):
        k = 0.0625 * part - 0.5625 * g_ref[at, right].astype(F32)
        return (g2_ref, part.astype(BF16)), (k_ref, k.astype(BF16))

    symmetric(lambda at, right: dot(g_ref[at, :], g_ref[:, right]), square)

    def rest(at, right, part):
        w = part + 1.6875 * g2_ref[at, right].astype(F32) - 2.4375 * g_ref[at, right].astype(F32)
        return ((w_ref, w.astype(BF16)),)

    symmetric(lambda at, right: dot(g2_ref[at, :], k_ref[:, right]), rest)


def polar_kernel(
    side_ref, mine_ref, other_ref, emb_ref, out_hbm, book_hbm,
    out_ref, book_ref, y_ref, z_ref, g_ref, g2_ref, k_ref, w_ref, full_ref, sems,
):
    side = side_ref[0]
    for rows_ref, at in ((mine_ref, side), (other_ref, 1 - side)):
        for q in range(HALF):
            here = pl.ds((q % QUARTER) * DS, DS)
            left = (q // QUARTER) * D
            y_ref[pl.ds(pl.multiple_of((2 * q + at) * DS, DS), DS), :] = rows_ref[here, left : left + D]
            left = 2 * D + (q // QUARTER) * K
            book_ref[2 * q + at] = rows_ref[here, left : left + K]

    copies = [pltpu.make_async_copy(book_ref, book_hbm, sems.at[0])]
    copies[0].start()

    squares = 0.0
    for i in range(PARTS):
        at, right = slice(i * PART, (i + 1) * PART), slice(i * PART, D)
        part = dot(y_ref[at, :], y_ref[right, :], NT)
        full_ref[at, right] = part
        squares = squares + jnp.sum(part[:, :PART] * part[:, :PART], keepdims=True)
        if i < PARTS - 1:
            squares = squares + 2.0 * jnp.sum(part[:, PART:] * part[:, PART:], keepdims=True)
    norm_square = jnp.sqrt(squares) + EPSILON
    scale = lax.rsqrt(norm_square)
    shrink = 1.0 / norm_square

    symmetric(
        lambda at, right: full_ref[at, right],
        lambda at, right, part: ((g_ref, (part * shrink).astype(BF16)),),
    )
    two_steps(g_ref, g2_ref, k_ref, w_ref)
    for i in range(2):
        at = slice(i * (D // 2), (i + 1) * (D // 2))
        part = 2.25 * y_ref[at, :].astype(F32) + dot(w_ref[at, :], y_ref[...])
        z_ref[at, :] = (scale * part).astype(BF16)

    symmetric(
        lambda at, right: dot(z_ref[at, :], z_ref[right, :], NT),
        lambda at, right, part: ((g_ref, part.astype(BF16)),),
    )
    turned = dot(emb_ref[...], z_ref[...], NT)
    two_steps(g_ref, g2_ref, k_ref, w_ref)
    for i in range(2):
        at = slice(i * MINE, (i + 1) * MINE)
        part = 2.25 * turned[at] + dot(turned[at].astype(BF16), w_ref[...])
        out_ref[at, :] = part.astype(BF16)
        rows = pl.ds(i * MINE, MINE)
        copies.append(pltpu.make_async_copy(out_ref.at[rows], out_hbm.at[rows], sems.at[1 + i]))
        copies[-1].start()
    for copy in copies:
        copy.wait()


def finish(side, mine, other, embeddings):
    return pl.pallas_call(
        polar_kernel,
        out_shape=(
            jax.ShapeDtypeStruct((TOK, D), BF16),
            jax.ShapeDtypeStruct((SUBS, DS, K), BF16),
        ),
        in_specs=[SMEM] + [VMEM] * 3,
        out_specs=(pl.BlockSpec(memory_space=pl.ANY),) * 2,
        scratch_shapes=[
            pltpu.VMEM((TOK, D), BF16),
            pltpu.VMEM((SUBS, DS, K), BF16),
            pltpu.VMEM((D, D), BF16),
            pltpu.VMEM((D, D), BF16),
            pltpu.VMEM((D, D), BF16),
            pltpu.VMEM((D, D), BF16),
            pltpu.VMEM((D, D), BF16),
            pltpu.VMEM((D, D), BF16),
            pltpu.VMEM((D, D), F32),
            pltpu.SemaphoreType.DMA((3,)),
        ],
        compiler_params=pltpu.CompilerParams(vmem_limit_bytes=36 * MIB),
        cost_estimate=pl.CostEstimate(flops=20 * 10**9, bytes_accessed=8 * 10**6, transcendentals=0),
        name="polar",
    )(side, mine, other, embeddings)


def local(embeddings, rotation, pq_codes, codebook):
    codes = pq_codes.T
    core = lax.axis_index("core")
    mine, other = jnp.full((1,), core, jnp.int32), jnp.full((1,), 1 - core, jnp.int32)

    theirs = lax.dynamic_index_in_dim(codebook, 1 - core, 0, keepdims=False)
    other_book = gather(theirs, ROW, HALF).reshape(HALF * DS, K)
    other_book, box = lax.optimization_barrier((other_book, lax.axis_index(BOX)))
    table = tables(embeddings, rotation, codes)
    mine_book = swap(other_book)
    sent = crosses(other, embeddings, codes, other_book, table)
    sent, mine_book = lax.optimization_barrier((sent, mine_book))
    got = swap(sent)
    kept = crosses(mine, embeddings, codes, mine_book, table)

    pair = (got.astype(F32) + kept.astype(F32)).astype(BF16)
    boxed = spread(pair.reshape(16, 16, WIDE), BOX)
    counted = boxed[:8, BACK:].reshape(2, 2, K)
    counted = counted[:, 0] + LOW * counted[:, 1]
    rest = jnp.floor(counted * (1.0 / LOW))
    high = jnp.floor(rest * (1.0 / LOW))
    digits = jnp.concatenate([counted - LOW * rest, rest - LOW * high, high], axis=0)
    digits = jnp.pad(digits.reshape(12, 128), ((0, 4), (0, 0)))
    packed = jnp.concatenate([boxed[:, :BACK], digits], axis=1).astype(BF16)
    packed = total(packed, 0).astype(BF16)
    summed = total(packed, 1)
    summed, mine_book, box = lax.optimization_barrier((summed, mine_book, box))

    counted = summed[:12, BACK:].reshape(3, 2, K)
    counted = counted[0] + LOW * counted[1] + (LOW * LOW) * counted[2]
    fresh = []
    for half in range(2):
        old = lax.dynamic_slice_in_dim(mine_book, box * DS + MINE * half, DS, 0).astype(F32)
        sums = summed[:, 2 * D + K * half : 2 * D + K * half + K]
        count = counted[half : half + 1]
        fresh.append(jnp.where(count > 0, sums / jnp.maximum(count, 1.0), old))
    own = jnp.concatenate([summed[:, : 2 * D]] + fresh, axis=1).astype(BF16)

    rows = gather(own, BOX, 16).reshape(MINE, BACK)
    rerotated, new_codebook = finish(mine, rows, swap(rows), embeddings)
    return (new_codebook, rerotated)


def solution(mesh):
    split = Mesh(mesh.devices.reshape(4, 2, 2, 4, 4, 2), AXES)
    placed = (P(AXES, None), P(), P(AXES, None), P(ROW, None, None))
    return jax.shard_map(
        local, mesh=split, in_specs=placed, out_specs=(P(), P(AXES, None)), check_vma=False
    )
```

```python
import jax
import jax.numpy as jnp
from jax import lax
from jax.experimental import pallas as pl
from jax.experimental.pallas import tpu as pltpu
from jax.sharding import Mesh, PartitionSpec as P

EPSILON = 1e-06
F32 = jnp.float32
BF16 = jnp.bfloat16

AXES = ("yh", "yl", "core", "x", "zh", "zl")
ROW = ("x", "zh", "zl")
BOX = ("x", "yl", "zl")

D = 1024
SUBS = 64
HALF = SUBS // 2
QUARTER = SUBS // 4
DS = 16
K = 256
TOK = 512
MINE = TOK // 2
LOW = 64.0
BACK = 2 * D + 2 * K
WIDE = BACK + 128

NN = (((1,), (0,)), ((), ()))
NT = (((1,), (1,)), ((), ()))
MIB = 1024 * 1024
VMEM = pl.BlockSpec(memory_space=pltpu.VMEM)
SMEM = pl.BlockSpec(memory_space=pltpu.SMEM)


def dot(a, b, dims=NN):
    return lax.dot_general(a, b, dims, preferred_element_type=F32)


def far_groups(turn):
    groups = []
    for yl in range(2):
        for core in range(2):
            for x in range(4):
                for other in range(4):
                    for zl in range(2):
                        along_y = core != turn
                        places = [(i, other) if along_y else (other, i) for i in range(4)]
                        groups.append(
                            [((((yh * 2 + yl) * 2 + core) * 4 + x) * 4 + zh) * 2 + zl for yh, zh in places]
                        )
    return groups


def box_groups():
    groups = []
    for core in range(2):
        for y in range(core, 8, 2):
            for z in range(core, 8, 2):
                groups.append(
                    [
                        (((y + yl) % 8 * 2 + core) * 4 + x) * 8 + (z + zl) % 8
                        for x in range(4)
                        for yl in range(2)
                        for zl in range(2)
                    ]
                )
    return groups


def gather(value, axes, peers, groups=None):
    spreadout = jnp.broadcast_to(value[None], (peers,) + value.shape)
    return lax.all_to_all(spreadout, axes, 0, 0, axis_index_groups=groups, tiled=True)


def spread(parts, axes, groups=None):
    got = lax.all_to_all(parts, axes, 0, 0, axis_index_groups=groups, tiled=True)
    return jnp.sum(got.astype(F32), axis=0)


def total(value, turn):
    return jnp.sum(gather(value, AXES, 4, far_groups(turn)).astype(F32), axis=0)


def swap(value):
    return lax.ppermute(value, "core", [(0, 1), (1, 0)])


def picks(codes_ref, sub):
    row = codes_ref[pl.ds(sub, 1), :].astype(jnp.int16)
    levels = lax.broadcasted_iota(jnp.int32, (K, TOK), 0).astype(jnp.int16)
    return jnp.where(levels == row, jnp.ones((), BF16), jnp.zeros((), BF16))


def tables_kernel(emb_hbm, rot_hbm, codes_hbm, out_ref, emb_ref, rot_ref, codes_ref, sems):
    copies = [
        pltpu.make_async_copy(source, target, sems.at[i])
        for i, (source, target) in enumerate(((emb_hbm, emb_ref), (rot_hbm, rot_ref), (codes_hbm, codes_ref)))
    ]
    for copy in copies:
        copy.start()
    lane = lax.broadcasted_iota(jnp.int32, (K, 128), 1) // DS
    line = lax.broadcasted_iota(jnp.int32, (DS, 128), 0)
    for copy in copies:
        copy.wait()

    rotated = dot(emb_ref[...], rot_ref[...]).astype(BF16)
    ones = jnp.ones((TOK, 128), BF16)

    def group(g):
        right = jnp.concatenate([rotated[:, 128 * g : 128 * g + 128], ones], axis=1)
        sums = jnp.zeros((K, 128), F32)
        counts = jnp.zeros((K, 128), F32)
        for place in range(8):
            both = dot(picks(codes_ref, 8 * g + place), right)
            sums = jnp.where(lane == place, both[:, :128], sums)
            counts = jnp.where(lane == place, both[:, 128:], counts)
        return sums.T, counts.T

    for g in range(4):
        made = [group(g), group(g + 4)]
        for place in range(8):
            here = slice(DS * place, DS * place + DS)
            at = pl.ds((4 * g + place // 2) * DS, DS)
            digits = jnp.zeros((DS, 128), F32)
            for half, (sums, counts) in enumerate(made):
                out_ref[place % 2, at, K * half : K * half + K] = sums[here].astype(BF16)
                count = counts[here]
                high = jnp.floor(count * (1.0 / LOW))
                low = count - LOW * high
                parts = (low[:, :128], low[:, 128:], high[:, :128], high[:, 128:])
                for row, part in enumerate(parts):
                    digits = jnp.where(line == 4 * half + row, part, digits)
            out_ref[place % 2, at, 2 * K :] = digits.astype(BF16)


def tables(embeddings, rotation, codes):
    return pl.pallas_call(
        tables_kernel,
        out_shape=jax.ShapeDtypeStruct((2, MINE, 2 * K + 128), BF16),
        in_specs=[pl.BlockSpec(memory_space=pl.ANY)] * 3,
        out_specs=VMEM,
        scratch_shapes=[
            pltpu.VMEM((TOK, D), BF16),
            pltpu.VMEM((D, D), BF16),
            pltpu.VMEM((SUBS, TOK), jnp.int32),
            pltpu.SemaphoreType.DMA((3,)),
        ],
        compiler_params=pltpu.CompilerParams(vmem_limit_bytes=53 * MIB),
        cost_estimate=pl.CostEstimate(flops=8 * 10**9, bytes_accessed=4 * 10**6, transcendentals=0),
        name="tables",
    )(embeddings, rotation, codes)


def cross_kernel(side_ref, emb_ref, codes_ref, book_ref, table_ref, out_ref, rebuilt_ref):
    side = side_ref[0]

    def step(q, carry):
        at = pl.ds(pl.multiple_of(q * DS, DS), DS)
        rebuilt_ref[at, :] = dot(book_ref[at, :], picks(codes_ref, 2 * q + side)).astype(BF16)
        return carry

    lax.fori_loop(0, HALF, step, 0, unroll=32)
    part = dot(rebuilt_ref[...], emb_ref[...])
    out_ref[:, :D] = part[:MINE].astype(BF16)
    out_ref[:, D : 2 * D] = part[MINE:].astype(BF16)
    out_ref[:, 2 * D :] = table_ref[side]


def crosses(side, embeddings, codes, book, table):
    return pl.pallas_call(
        cross_kernel,
        out_shape=jax.ShapeDtypeStruct((MINE, WIDE), BF16),
        in_specs=[SMEM] + [VMEM] * 4,
        out_specs=VMEM,
        scratch_shapes=[pltpu.VMEM((TOK, TOK), BF16)],
        compiler_params=pltpu.CompilerParams(vmem_limit_bytes=16 * MIB),
        cost_estimate=pl.CostEstimate(flops=4 * 10**9, bytes_accessed=4 * 10**6, transcendentals=0),
        name="crosses",
    )(side, embeddings, codes, book, table)


PARTS = 4
PART = D // PARTS


def symmetric(product, store):
    for i in range(PARTS):
        at, right = slice(i * PART, (i + 1) * PART), slice(i * PART, D)
        for target, value in store(at, right, product(at, right)):
            target[at, right] = value
            if i < PARTS - 1:
                target[(i + 1) * PART :, at] = value[:, PART:].T


def two_steps(g_ref, g2_ref, k_ref, w_ref):
    def square(at, right, part):
        k = 0.0625 * part - 0.5625 * g_ref[at, right].astype(F32)
        return (g2_ref, part.astype(BF16)), (k_ref, k.astype(BF16))

    symmetric(lambda at, right: dot(g_ref[at, :], g_ref[:, right]), square)

    def rest(at, right, part):
        w = part + 1.6875 * g2_ref[at, right].astype(F32) - 2.4375 * g_ref[at, right].astype(F32)
        return ((w_ref, w.astype(BF16)),)

    symmetric(lambda at, right: dot(g2_ref[at, :], k_ref[:, right]), rest)


def polar_kernel(
    side_ref, mine_ref, other_ref, emb_ref, out_hbm, book_hbm,
    out_ref, book_ref, y_ref, z_ref, g_ref, g2_ref, k_ref, w_ref, full_ref, sems,
):
    side = side_ref[0]
    for rows_ref, at in ((mine_ref, side), (other_ref, 1 - side)):
        for q in range(HALF):
            here = pl.ds((q % QUARTER) * DS, DS)
            left = (q // QUARTER) * D
            y_ref[pl.ds(pl.multiple_of((2 * q + at) * DS, DS), DS), :] = rows_ref[here, left : left + D]
            left = 2 * D + (q // QUARTER) * K
            book_ref[2 * q + at] = rows_ref[here, left : left + K]

    copies = [pltpu.make_async_copy(book_ref, book_hbm, sems.at[0])]
    copies[0].start()

    squares = 0.0
    for i in range(PARTS):
        at, right = slice(i * PART, (i + 1) * PART), slice(i * PART, D)
        part = dot(y_ref[at, :], y_ref[right, :], NT)
        full_ref[at, right] = part
        squares = squares + jnp.sum(part[:, :PART] * part[:, :PART], keepdims=True)
        if i < PARTS - 1:
            squares = squares + 2.0 * jnp.sum(part[:, PART:] * part[:, PART:], keepdims=True)
    norm_square = jnp.sqrt(squares) + EPSILON
    scale = lax.rsqrt(norm_square)
    shrink = 1.0 / norm_square

    symmetric(
        lambda at, right: full_ref[at, right],
        lambda at, right, part: ((g_ref, (part * shrink).astype(BF16)),),
    )
    two_steps(g_ref, g2_ref, k_ref, w_ref)
    for i in range(2):
        at = slice(i * (D // 2), (i + 1) * (D // 2))
        part = 2.25 * y_ref[at, :].astype(F32) + dot(w_ref[at, :], y_ref[...])
        z_ref[at, :] = (scale * part).astype(BF16)

    symmetric(
        lambda at, right: dot(z_ref[at, :], z_ref[right, :], NT),
        lambda at, right, part: ((g_ref, part.astype(BF16)),),
    )
    turned = dot(emb_ref[...], z_ref[...], NT)
    two_steps(g_ref, g2_ref, k_ref, w_ref)
    for i in range(2):
        at = slice(i * MINE, (i + 1) * MINE)
        part = 2.25 * turned[at] + dot(turned[at].astype(BF16), w_ref[...])
        out_ref[at, :] = part.astype(BF16)
        rows = pl.ds(i * MINE, MINE)
        copies.append(pltpu.make_async_copy(out_ref.at[rows], out_hbm.at[rows], sems.at[1 + i]))
        copies[-1].start()
    for copy in copies:
        copy.wait()


def finish(side, mine, other, embeddings):
    return pl.pallas_call(
        polar_kernel,
        out_shape=(
            jax.ShapeDtypeStruct((TOK, D), BF16),
            jax.ShapeDtypeStruct((SUBS, DS, K), BF16),
        ),
        in_specs=[SMEM] + [VMEM] * 3,
        out_specs=(pl.BlockSpec(memory_space=pl.ANY),) * 2,
        scratch_shapes=[
            pltpu.VMEM((TOK, D), BF16),
            pltpu.VMEM((SUBS, DS, K), BF16),
            pltpu.VMEM((D, D), BF16),
            pltpu.VMEM((D, D), BF16),
            pltpu.VMEM((D, D), BF16),
            pltpu.VMEM((D, D), BF16),
            pltpu.VMEM((D, D), BF16),
            pltpu.VMEM((D, D), BF16),
            pltpu.VMEM((D, D), F32),
            pltpu.SemaphoreType.DMA((3,)),
        ],
        compiler_params=pltpu.CompilerParams(vmem_limit_bytes=36 * MIB),
        cost_estimate=pl.CostEstimate(flops=20 * 10**9, bytes_accessed=8 * 10**6, transcendentals=0),
        name="polar",
    )(side, mine, other, embeddings)


def local(embeddings, rotation, pq_codes, codebook):
    codes = pq_codes.T
    core = lax.axis_index("core")
    mine, other = jnp.full((1,), core, jnp.int32), jnp.full((1,), 1 - core, jnp.int32)

    theirs = lax.dynamic_index_in_dim(codebook, 1 - core, 0, keepdims=False)
    other_book = gather(theirs, ROW, HALF).reshape(HALF * DS, K)
    box = lax.axis_index(BOX) ^ (3 * core)
    other_book, box = lax.optimization_barrier((other_book, box))
    table = tables(embeddings, rotation, codes)
    mine_book = swap(other_book)
    sent = crosses(other, embeddings, codes, other_book, table)
    sent, mine_book = lax.optimization_barrier((sent, mine_book))
    got = swap(sent)
    kept = crosses(mine, embeddings, codes, mine_book, table)

    pair = (got.astype(F32) + kept.astype(F32)).astype(BF16)
    boxed = spread(pair.reshape(16, 16, WIDE), AXES, box_groups())
    counted = boxed[:8, BACK:].reshape(2, 2, K)
    counted = counted[:, 0] + LOW * counted[:, 1]
    rest = jnp.floor(counted * (1.0 / LOW))
    high = jnp.floor(rest * (1.0 / LOW))
    digits = jnp.concatenate([counted - LOW * rest, rest - LOW * high, high], axis=0)
    digits = jnp.pad(digits.reshape(12, 128), ((0, 4), (0, 0)))
    packed = jnp.concatenate([boxed[:, :BACK], digits], axis=1).astype(BF16)
    packed = total(packed, 0).astype(BF16)
    summed = total(packed, 1)
    summed, mine_book, box = lax.optimization_barrier((summed, mine_book, box))

    counted = summed[:12, BACK:].reshape(3, 2, K)
    counted = counted[0] + LOW * counted[1] + (LOW * LOW) * counted[2]
    fresh = []
    for half in range(2):
        old = lax.dynamic_slice_in_dim(mine_book, box * DS + MINE * half, DS, 0).astype(F32)
        sums = summed[:, 2 * D + K * half : 2 * D + K * half + K]
        count = counted[half : half + 1]
        fresh.append(jnp.where(count > 0, sums / jnp.maximum(count, 1.0), old))
    own = jnp.concatenate([summed[:, : 2 * D]] + fresh, axis=1).astype(BF16)

    rows = gather(own, AXES, 16, box_groups()).reshape(MINE, BACK)
    rerotated, new_codebook = finish(mine, rows, swap(rows), embeddings)
    return (new_codebook, rerotated)


def solution(mesh):
    split = Mesh(mesh.devices.reshape(4, 2, 2, 4, 4, 2), AXES)
    placed = (P(AXES, None), P(), P(AXES, None), P(ROW, None, None))
    return jax.shard_map(
        local, mesh=split, in_specs=placed, out_specs=(P(), P(AXES, None)), check_vma=False
    )
```

```python
import jax
import jax.numpy as jnp
from jax import lax
from jax.experimental import pallas as pl
from jax.experimental.pallas import tpu as pltpu
from jax.sharding import Mesh, PartitionSpec as P

EPSILON = 1e-06
F32 = jnp.float32
BF16 = jnp.bfloat16

AXES = ("yh", "yl", "core", "x", "zh", "zl")
ROW = ("x", "zh", "zl")
BOX = ("x", "yl", "zl")

D = 1024
SUBS = 64
HALF = SUBS // 2
QUARTER = SUBS // 4
DS = 16
K = 256
TOK = 512
MINE = TOK // 2
LOW = 64.0
BACK = 2 * D + 2 * K
WIDE = BACK + 128

NN = (((1,), (0,)), ((), ()))
NT = (((1,), (1,)), ((), ()))
MIB = 1024 * 1024
VMEM = pl.BlockSpec(memory_space=pltpu.VMEM)
SMEM = pl.BlockSpec(memory_space=pltpu.SMEM)


def dot(a, b, dims=NN):
    return lax.dot_general(a, b, dims, preferred_element_type=F32)


def far_groups(turn):
    groups = []
    for yl in range(2):
        for core in range(2):
            for x in range(4):
                for other in range(4):
                    for zl in range(2):
                        along_y = core == turn
                        places = [(i, other) if along_y else (other, i) for i in range(4)]
                        groups.append(
                            [((((yh * 2 + yl) * 2 + core) * 4 + x) * 4 + zh) * 2 + zl for yh, zh in places]
                        )
    return groups


def box_groups():
    groups = []
    for core in range(2):
        for y in range(core, 8, 2):
            for z in range(core, 8, 2):
                groups.append(
                    [
                        (((y + yl) % 8 * 2 + core) * 4 + x) * 8 + (z + zl) % 8
                        for x in range(4)
                        for yl in range(2)
                        for zl in range(2)
                    ]
                )
    return groups


def gather(value, axes, peers, groups=None):
    spreadout = jnp.broadcast_to(value[None], (peers,) + value.shape)
    return lax.all_to_all(spreadout, axes, 0, 0, axis_index_groups=groups, tiled=True)


def spread(parts, axes, groups=None):
    got = lax.all_to_all(parts, axes, 0, 0, axis_index_groups=groups, tiled=True)
    return jnp.sum(got.astype(F32), axis=0)


def total(value, turn):
    return jnp.sum(gather(value, AXES, 4, far_groups(turn)).astype(F32), axis=0)


def swap(value):
    return lax.ppermute(value, "core", [(0, 1), (1, 0)])


def picks(codes_ref, sub):
    row = codes_ref[pl.ds(sub, 1), :].astype(jnp.int16)
    levels = lax.broadcasted_iota(jnp.int32, (K, TOK), 0).astype(jnp.int16)
    return jnp.where(levels == row, jnp.ones((), BF16), jnp.zeros((), BF16))


def tables_kernel(emb_hbm, rot_hbm, codes_hbm, out_ref, emb_ref, rot_ref, codes_ref, sems):
    copies = [
        pltpu.make_async_copy(source, target, sems.at[i])
        for i, (source, target) in enumerate(((emb_hbm, emb_ref), (rot_hbm, rot_ref), (codes_hbm, codes_ref)))
    ]
    for copy in copies:
        copy.start()
    lane = lax.broadcasted_iota(jnp.int32, (K, 128), 1) // DS
    line = lax.broadcasted_iota(jnp.int32, (DS, 128), 0)
    for copy in copies:
        copy.wait()

    rotated = dot(emb_ref[...], rot_ref[...]).astype(BF16)
    ones = jnp.ones((TOK, 128), BF16)

    def group(g):
        right = jnp.concatenate([rotated[:, 128 * g : 128 * g + 128], ones], axis=1)
        sums = jnp.zeros((K, 128), F32)
        counts = jnp.zeros((K, 128), F32)
        for place in range(8):
            both = dot(picks(codes_ref, 8 * g + place), right)
            sums = jnp.where(lane == place, both[:, :128], sums)
            counts = jnp.where(lane == place, both[:, 128:], counts)
        return sums.T, counts.T

    for g in range(4):
        made = [group(g), group(g + 4)]
        for place in range(8):
            here = slice(DS * place, DS * place + DS)
            at = pl.ds((4 * g + place // 2) * DS, DS)
            digits = jnp.zeros((DS, 128), F32)
            for half, (sums, counts) in enumerate(made):
                out_ref[place % 2, at, K * half : K * half + K] = sums[here].astype(BF16)
                count = counts[here]
                high = jnp.floor(count * (1.0 / LOW))
                low = count - LOW * high
                parts = (low[:, :128], low[:, 128:], high[:, :128], high[:, 128:])
                for row, part in enumerate(parts):
                    digits = jnp.where(line == 4 * half + row, part, digits)
            out_ref[place % 2, at, 2 * K :] = digits.astype(BF16)


def tables(embeddings, rotation, codes):
    return pl.pallas_call(
        tables_kernel,
        out_shape=jax.ShapeDtypeStruct((2, MINE, 2 * K + 128), BF16),
        in_specs=[pl.BlockSpec(memory_space=pl.ANY)] * 3,
        out_specs=VMEM,
        scratch_shapes=[
            pltpu.VMEM((TOK, D), BF16),
            pltpu.VMEM((D, D), BF16),
            pltpu.VMEM((SUBS, TOK), jnp.int32),
            pltpu.SemaphoreType.DMA((3,)),
        ],
        compiler_params=pltpu.CompilerParams(vmem_limit_bytes=53 * MIB),
        cost_estimate=pl.CostEstimate(flops=8 * 10**9, bytes_accessed=4 * 10**6, transcendentals=0),
        name="tables",
    )(embeddings, rotation, codes)


def cross_kernel(side_ref, emb_ref, codes_ref, book_ref, table_ref, out_ref, rebuilt_ref):
    side = side_ref[0]

    def step(q, carry):
        at = pl.ds(pl.multiple_of(q * DS, DS), DS)
        rebuilt_ref[at, :] = dot(book_ref[at, :], picks(codes_ref, 2 * q + side)).astype(BF16)
        return carry

    lax.fori_loop(0, HALF, step, 0, unroll=32)
    part = dot(rebuilt_ref[...], emb_ref[...])
    out_ref[:, :D] = part[:MINE].astype(BF16)
    out_ref[:, D : 2 * D] = part[MINE:].astype(BF16)
    out_ref[:, 2 * D :] = table_ref[side]


def crosses(side, embeddings, codes, book, table):
    return pl.pallas_call(
        cross_kernel,
        out_shape=jax.ShapeDtypeStruct((MINE, WIDE), BF16),
        in_specs=[SMEM] + [VMEM] * 4,
        out_specs=VMEM,
        scratch_shapes=[pltpu.VMEM((TOK, TOK), BF16)],
        compiler_params=pltpu.CompilerParams(vmem_limit_bytes=16 * MIB),
        cost_estimate=pl.CostEstimate(flops=4 * 10**9, bytes_accessed=4 * 10**6, transcendentals=0),
        name="crosses",
    )(side, embeddings, codes, book, table)


PARTS = 4
PART = D // PARTS


def symmetric(product, store):
    for i in range(PARTS):
        at, right = slice(i * PART, (i + 1) * PART), slice(i * PART, D)
        for target, value in store(at, right, product(at, right)):
            target[at, right] = value
            if i < PARTS - 1:
                target[(i + 1) * PART :, at] = value[:, PART:].T


def two_steps(g_ref, g2_ref, k_ref, w_ref):
    def square(at, right, part):
        k = 0.0625 * part - 0.5625 * g_ref[at, right].astype(F32)
        return (g2_ref, part.astype(BF16)), (k_ref, k.astype(BF16))

    symmetric(lambda at, right: dot(g_ref[at, :], g_ref[:, right]), square)

    def rest(at, right, part):
        w = part + 1.6875 * g2_ref[at, right].astype(F32) - 2.4375 * g_ref[at, right].astype(F32)
        return ((w_ref, w.astype(BF16)),)

    symmetric(lambda at, right: dot(g2_ref[at, :], k_ref[:, right]), rest)


def polar_kernel(
    side_ref, mine_ref, other_ref, emb_ref, out_hbm, book_hbm,
    out_ref, book_ref, y_ref, z_ref, g_ref, g2_ref, k_ref, w_ref, full_ref, sems,
):
    side = side_ref[0]
    for rows_ref, at in ((mine_ref, side), (other_ref, 1 - side)):
        for q in range(HALF):
            here = pl.ds(pl.multiple_of(((q % QUARTER) ^ (3 * at)) * DS, DS), DS)
            left = (q // QUARTER) * D
            y_ref[pl.ds(pl.multiple_of((2 * q + at) * DS, DS), DS), :] = rows_ref[here, left : left + D]
            left = 2 * D + (q // QUARTER) * K
            book_ref[2 * q + at] = rows_ref[here, left : left + K]

    copies = [pltpu.make_async_copy(book_ref, book_hbm, sems.at[0])]
    copies[0].start()

    squares = 0.0
    for i in range(PARTS):
        at, right = slice(i * PART, (i + 1) * PART), slice(i * PART, D)
        part = dot(y_ref[at, :], y_ref[right, :], NT)
        full_ref[at, right] = part
        squares = squares + jnp.sum(part[:, :PART] * part[:, :PART], keepdims=True)
        if i < PARTS - 1:
            squares = squares + 2.0 * jnp.sum(part[:, PART:] * part[:, PART:], keepdims=True)
    norm_square = jnp.sqrt(squares) + EPSILON
    scale = lax.rsqrt(norm_square)
    shrink = 1.0 / norm_square

    symmetric(
        lambda at, right: full_ref[at, right],
        lambda at, right, part: ((g_ref, (part * shrink).astype(BF16)),),
    )
    two_steps(g_ref, g2_ref, k_ref, w_ref)
    for i in range(2):
        at = slice(i * (D // 2), (i + 1) * (D // 2))
        part = 2.25 * y_ref[at, :].astype(F32) + dot(w_ref[at, :], y_ref[...])
        z_ref[at, :] = (scale * part).astype(BF16)

    symmetric(
        lambda at, right: dot(z_ref[at, :], z_ref[right, :], NT),
        lambda at, right, part: ((g_ref, part.astype(BF16)),),
    )
    turned = dot(emb_ref[...], z_ref[...], NT)
    two_steps(g_ref, g2_ref, k_ref, w_ref)
    for i in range(2):
        at = slice(i * MINE, (i + 1) * MINE)
        part = 2.25 * turned[at] + dot(turned[at].astype(BF16), w_ref[...])
        out_ref[at, :] = part.astype(BF16)
        rows = pl.ds(i * MINE, MINE)
        copies.append(pltpu.make_async_copy(out_ref.at[rows], out_hbm.at[rows], sems.at[1 + i]))
        copies[-1].start()
    for copy in copies:
        copy.wait()


def finish(side, mine, other, embeddings):
    return pl.pallas_call(
        polar_kernel,
        out_shape=(
            jax.ShapeDtypeStruct((TOK, D), BF16),
            jax.ShapeDtypeStruct((SUBS, DS, K), BF16),
        ),
        in_specs=[SMEM] + [VMEM] * 3,
        out_specs=(pl.BlockSpec(memory_space=pl.ANY),) * 2,
        scratch_shapes=[
            pltpu.VMEM((TOK, D), BF16),
            pltpu.VMEM((SUBS, DS, K), BF16),
            pltpu.VMEM((D, D), BF16),
            pltpu.VMEM((D, D), BF16),
            pltpu.VMEM((D, D), BF16),
            pltpu.VMEM((D, D), BF16),
            pltpu.VMEM((D, D), BF16),
            pltpu.VMEM((D, D), BF16),
            pltpu.VMEM((D, D), F32),
            pltpu.SemaphoreType.DMA((3,)),
        ],
        compiler_params=pltpu.CompilerParams(vmem_limit_bytes=36 * MIB),
        cost_estimate=pl.CostEstimate(flops=20 * 10**9, bytes_accessed=8 * 10**6, transcendentals=0),
        name="polar",
    )(side, mine, other, embeddings)


def local(embeddings, rotation, pq_codes, codebook):
    codes = pq_codes.T
    core = lax.axis_index("core")
    mine, other = jnp.full((1,), core, jnp.int32), jnp.full((1,), 1 - core, jnp.int32)

    theirs = lax.dynamic_index_in_dim(codebook, 1 - core, 0, keepdims=False)
    other_book = gather(theirs, ROW, HALF).reshape(HALF * DS, K)
    box = lax.axis_index(BOX) ^ (3 * core)
    other_book, box = lax.optimization_barrier((other_book, box))
    table = tables(embeddings, rotation, codes)
    mine_book = swap(other_book)
    sent = crosses(other, embeddings, codes, other_book, table)
    sent, mine_book = lax.optimization_barrier((sent, mine_book))
    got = swap(sent)
    kept = crosses(mine, embeddings, codes, mine_book, table)

    pair = (got.astype(F32) + kept.astype(F32)).astype(BF16)
    boxed = spread(pair.reshape(16, 16, WIDE), AXES, box_groups())
    counted = boxed[:8, BACK:].reshape(2, 2, K)
    counted = counted[:, 0] + LOW * counted[:, 1]
    rest = jnp.floor(counted * (1.0 / LOW))
    high = jnp.floor(rest * (1.0 / LOW))
    digits = jnp.concatenate([counted - LOW * rest, rest - LOW * high, high], axis=0)
    digits = jnp.pad(digits.reshape(12, 128), ((0, 4), (0, 0)))
    packed = jnp.concatenate([boxed[:, :BACK], digits], axis=1).astype(BF16)
    packed = total(packed, 0).astype(BF16)
    summed = total(packed, 1)
    summed, mine_book, box = lax.optimization_barrier((summed, mine_book, box))

    counted = summed[:12, BACK:].reshape(3, 2, K)
    counted = counted[0] + LOW * counted[1] + (LOW * LOW) * counted[2]
    fresh = []
    for half in range(2):
        old = lax.dynamic_slice_in_dim(mine_book, box * DS + MINE * half, DS, 0).astype(F32)
        sums = summed[:, 2 * D + K * half : 2 * D + K * half + K]
        count = counted[half : half + 1]
        fresh.append(jnp.where(count > 0, sums / jnp.maximum(count, 1.0), old))
    own = jnp.concatenate([summed[:, : 2 * D]] + fresh, axis=1).astype(BF16)

    rows = gather(own, BOX, 16).reshape(MINE, BACK)
    rerotated, new_codebook = finish(mine, rows, swap(rows), embeddings)
    return (new_codebook, rerotated)


def solution(mesh):
    split = Mesh(mesh.devices.reshape(4, 2, 2, 4, 4, 2), AXES)
    placed = (P(AXES, None), P(), P(AXES, None), P(ROW, None, None))
    return jax.shard_map(
        local, mesh=split, in_specs=placed, out_specs=(P(), P(AXES, None)), check_vma=False
    )
```
